256 devices in a mesh: ep: 64 (over y, x_lo, z), dp: 4 (over x_hi, core).
Axes of the slice: x: 4 (x_hi: 2, x_lo: 2; x = x_hi * 2 + x_lo), y: 4, z: 8, core: 2. Of those that a mesh axis runs over, the one named last changes fastest.
Arguments:
- tokens: bfloat16 [8192, 7168], P('ep', 'dp'), may hold values from -6 to 6
- cotangent: bfloat16 [8192, 7168], P('ep', 'dp'), may hold values from -0.29882812 to 0.29882812
- gate_prob: bfloat16 [8192, 2], P('ep'), may hold values from 0.099609375 to 1
- expert_ids: int32 [8192, 2], P('ep'), may hold values from 0 to 31, all different within a row; in each aligned block of 128 rows (0 to 127, 128 to 255, ...) at most 10 rows name the same one
- w_up: bfloat16 [64, 7168, 512], P('ep', 'dp'), may hold values from -0.0625 to 0.0625
- w_down: bfloat16 [64, 512, 7168], P('ep', None, 'dp'), may hold values from -0.1875 to 0.1875
Outputs:
- grad_tokens: bfloat16 [8192, 7168], P('ep', 'dp')
- grad_gate: float32 [8192, 2], P('ep')
- grad_up: bfloat16 [64, 7168, 512], P('ep', 'dp')
- grad_down: bfloat16 [64, 512, 7168], P('ep', None, 'dp')
The draws below stay inside these ranges and needn't reach their ends.
Inputs may be any that keep to these rules, and one draw needn't show every extreme that they name: `expert_ids`: the 2 experts of one token differ. Among the routes of the tokens of one index of ep (aligned blocks of 128 tokens), no expert is named more than 10 times, a bound that some block reaches.
All inputs are finite; a program needn't handle non-finite values.
Results may differ from the reference program's by a relative error of at most 0.012.
Values may be sent and summed in bfloat16 or wider, within the bound.
A program may use at most 128 MiB of HBM per device.

```python
import math
import jax
import jax.numpy as jnp
import numpy as np
from jax import lax

D = 7168
FF = 1024
TOP = 2
TOK_DEV = 128
EXPERTS = 32
HALF = 512
CAP = 10
TOKENS = 8192
N_EP = 64


def level_of(key, extent, pieces, smallest, high):
    loudness, own = 1.0, jax.random.fold_in(key, 6)
    for position, shards_of in pieces:
        heights = jnp.exp(jax.random.uniform(jax.random.fold_in(own, position), (shards_of,), jnp.float32, smallest / len(pieces), high / len(pieces)))
        loudness = loudness * jnp.repeat(heights, extent[position] // shards_of).reshape([-1 if axis == position else 1 for axis in range(len(extent))])
    return loudness


def shared_out(stream_key, own, number, rows, count, top, limit, slope):
    ranking = jax.random.permutation(stream_key, count)
    heavy_load, common = load_shares(count, rows * top, limit, slope, True), load_shares(count, rows * top, limit, slope, False)
    places = jnp.arange(count)

    def named(sizes, turn):
        used = int((sizes > 0).sum())
        fixed = max(1, used // 4)
        shifted = fixed + (places - fixed + turn * (used - fixed)) % max(1, count - fixed)
        return jnp.zeros((count,), jnp.int32).at[ranking[jnp.where(places < fixed, places, shifted)]].set(jnp.asarray(sizes, jnp.int32))

    sizes = jnp.where(number % 4 == 0, named(heavy_load, number // 4), named(common, number - number // 4 - 1))
    mixed = jax.random.permutation(jax.random.fold_in(own, 3), count)
    donor, sink = mixed[0:count // 2 * 2:2], mixed[1:count // 2 * 2:2]
    margin = jnp.minimum(sizes[donor] - 1, limit - sizes[sink]) // 2
    margin = jnp.where((donor == ranking[0]) | (sink == ranking[0]) | (sizes[sink] == 0), 0, jnp.maximum(margin, 0))
    shifted = jax.random.randint(jax.random.fold_in(own, 4), (count // 2,), 0, 1 << 20) % (margin + 1)
    sizes = sizes.at[donor].add(-shifted).at[sink].add(shifted)
    labels = jnp.searchsorted(jnp.cumsum(sizes), jnp.arange(rows * top), side="right").astype(jnp.int32)
    grid = labels.reshape(top, rows).T
    grid = grid[jax.random.permutation(jax.random.fold_in(own, 1), rows)]
    turn = jax.random.randint(jax.random.fold_in(own, 2), (rows, 1), 0, top)
    return jnp.take_along_axis(grid, (jnp.arange(top)[None, :] + turn) % top, axis=1)


def load_shares(amount, total, reach, slope, full):
    portions = [(1 << 20) // math.isqrt(grade ** slope) + 1 for grade in range(1, amount + 1)]
    largest = reach if full else min(reach, max(-(-total // amount), total * portions[0] // sum(portions)))
    least = 1 if total - largest >= amount - 1 else 0
    given, spare = [largest] + [least] * (amount - 1), total - largest - least * (amount - 1)
    while spare > 0:
        candidates = [i for i in range(1, amount) if given[i] < largest] or [i for i in range(1, amount) if given[i] < reach]
        whole, remaining = sum([portions[i] for i in candidates]), spare
        for i in candidates:
            more = min(reach - given[i], max(1, remaining * portions[i] // whole), spare)
            given[i] = given[i] + more
            spare = spare - more
    return np.array(given)


def scatter_about(own_key, dims, deviation, most, cuts=(), kind=jnp.bfloat16):
    drawn = jax.random.normal(own_key, dims, jnp.float32) * deviation
    if len(cuts) > 0:
        drawn = level_of(own_key, dims, cuts, -0.22, 0.18) * drawn
    return jnp.clip(drawn, min=-most, max=most).astype(kind)


def setup_inputs(seed: int = 0) -> dict:
    streams_of = jax.random.split(jax.random.key(seed), 7)
    tokens = scatter_about(streams_of[0], (TOKENS, D), 1.0, 6.0, ((0, 64), (1, 4)))
    cotangent = scatter_about(streams_of[1], (TOKENS, D), 0.05, 0.29882812, ((0, 64), (1, 4)))
    gate_prob = jnp.clip(0.099609375 + 0.9003906 * jax.random.uniform(streams_of[2], (TOKENS, TOP), jnp.float32) ** level_of(streams_of[2], (TOKENS, TOP), ((0, 64),), -0.2, 0.2), 0.099609375, 1.0).astype(jnp.bfloat16)
    expert_ids_keys = jax.random.split(jax.random.fold_in(streams_of[3], 1), TOKENS // TOK_DEV)
    expert_ids_turns = jax.random.permutation(jax.random.fold_in(streams_of[3], 3), TOKENS // TOK_DEV)
    expert_ids = jax.vmap(lambda own, number: shared_out(jax.random.fold_in(streams_of[3], 2), own, number, TOK_DEV, EXPERTS, TOP, CAP, 2))(expert_ids_keys, expert_ids_turns).reshape((TOKENS, TOP))
    w_up = scatter_about(streams_of[4], (2 * EXPERTS, D, HALF), D ** -0.5, 0.0625, ((0, 64), (1, 4)))
    w_down = scatter_about(streams_of[5], (2 * EXPERTS, HALF, D), FF ** -0.5, 0.1875, ((0, 64), (2, 4)))
    return {"tokens": tokens, "cotangent": cotangent, "gate_prob": gate_prob, "expert_ids": expert_ids, "w_up": w_up, "w_down": w_down}


def silu_slope(preact):
    sigmoid_val = jax.nn.sigmoid(preact)
    return sigmoid_val * (1.0 + preact * (1.0 - sigmoid_val))


def reference(tokens, cotangent, gate_prob, expert_ids, w_up, w_down):
    route_total = TOKENS * TOP
    flat_ids = expert_ids.reshape(-1).astype(jnp.int32)
    expert_range = jnp.arange(EXPERTS, dtype=jnp.int32)
    one_hot = (flat_ids[:, None] == expert_range[None, :]).astype(jnp.int32)
    one_hot = one_hot.reshape(N_EP, TOK_DEV * TOP, EXPERTS)
    slot_rank = jnp.sum((jnp.cumsum(one_hot, axis=1) - one_hot) * one_hot, axis=2).reshape(-1)
    route_index = jnp.arange(route_total, dtype=jnp.int32)
    source_device = route_index // (TOK_DEV * TOP)
    slot_table = jnp.full((EXPERTS, N_EP * CAP), -1, jnp.int32)
    slot_table = slot_table.at[flat_ids, source_device * CAP + slot_rank].set(route_index)
    up_blocks = w_up.reshape(EXPERTS, 2, D, HALF)
    down_blocks = w_down.reshape(EXPERTS, 2, HALF, D)
    gate_flat = gate_prob.reshape(-1).astype(jnp.float32)

    def per_expert(dx_total, inputs):
        row_ids, up_pair, down_pair = inputs
        row_valid = row_ids >= 0
        safe_ids = jnp.where(row_valid, row_ids, 0)
        token_row = safe_ids // TOP
        zero_bf = jnp.zeros((), tokens.dtype)
        row_tokens = jnp.where(row_valid[:, None], tokens[token_row], zero_bf)
        row_cot = jnp.where(row_valid[:, None], cotangent[token_row], zero_bf)
        row_gates = jnp.where(row_valid, gate_flat[safe_ids], jnp.zeros((), jnp.float32))
        full_up = jnp.concatenate([up_pair[0], up_pair[1]], axis=1)
        full_down = jnp.concatenate([down_pair[0], down_pair[1]], axis=0)
        preact = jnp.dot(row_tokens, full_up, preferred_element_type=jnp.float32)
        activations = jax.nn.silu(preact).astype(jnp.bfloat16)
        upstream = jnp.dot(row_cot, full_down.T, preferred_element_type=jnp.float32)
        products = activations.astype(jnp.float32) * upstream
        score_low = jnp.sum(products[:, :HALF], axis=1).astype(jnp.bfloat16)
        score_high = jnp.sum(products[:, HALF:], axis=1).astype(jnp.bfloat16)
        scores = score_low.astype(jnp.float32) + score_high.astype(jnp.float32)
        grad_preact = (row_gates[:, None] * upstream * silu_slope(preact)).astype(jnp.bfloat16)
        scaled_cot = (row_gates[:, None] * row_cot.astype(jnp.float32)).astype(jnp.bfloat16)
        part_low = jnp.dot(grad_preact[:, :HALF], full_up[:, :HALF].T, preferred_element_type=jnp.float32).astype(jnp.bfloat16)
        part_high = jnp.dot(grad_preact[:, HALF:], full_up[:, HALF:].T, preferred_element_type=jnp.float32).astype(jnp.bfloat16)
        route_sum = (part_low.astype(jnp.float32) + part_high.astype(jnp.float32)).astype(jnp.bfloat16)
        dx_rows = lax.optimization_barrier(route_sum).astype(jnp.float32)
        dx_total = dx_total.at[token_row].add(jnp.where(row_valid[:, None], dx_rows, jnp.zeros((), jnp.float32)))
        source_of = safe_ids // (TOK_DEV * TOP)
        to_replica = row_valid & (source_of >= N_EP // 2)
        keep_owner = row_valid & jnp.logical_not(to_replica)

        def weight_grads(row_mask):
            masked_tokens = jnp.where(row_mask[:, None], row_tokens, zero_bf)
            masked_acts = jnp.where(row_mask[:, None], activations, jnp.zeros((), activations.dtype))
            grad_in = jnp.dot(masked_tokens.T, grad_preact, preferred_element_type=jnp.float32)
            grad_out = jnp.dot(masked_acts.T, scaled_cot, preferred_element_type=jnp.float32)
            return grad_in, grad_out

        owner_up, owner_down = weight_grads(keep_owner)
        replica_up, replica_down = weight_grads(to_replica)
        replica_up = lax.optimization_barrier(replica_up.astype(jnp.bfloat16)).astype(jnp.float32)
        replica_down = lax.optimization_barrier(replica_down.astype(jnp.bfloat16)).astype(jnp.float32)
        grad_up = (owner_up + replica_up).astype(jnp.bfloat16)
        grad_down = (owner_down + replica_down).astype(jnp.bfloat16)
        grad_up_pair = jnp.stack([grad_up[:, :HALF], grad_up[:, HALF:]])
        grad_down_pair = jnp.stack([grad_down[:HALF], grad_down[HALF:]])
        return dx_total, (scores, grad_up_pair, grad_down_pair)

    dx_total, outputs = lax.scan(per_expert, jnp.zeros((TOKENS, D), jnp.float32), (slot_table, up_blocks, down_blocks))
    scores, grad_up, grad_down = outputs
    target_ids = jnp.where(slot_table >= 0, slot_table, route_total).reshape(-1)
    gate_grad = jnp.zeros((route_total,), jnp.float32).at[target_ids].set(scores.reshape(-1), mode="drop")
    return (dx_total.astype(jnp.bfloat16), gate_grad.reshape(TOKENS, TOP), grad_up.reshape(2 * EXPERTS, D, HALF), grad_down.reshape(2 * EXPERTS, HALF, D))
```

```python
import functools

import jax
import jax.numpy as jnp
from jax import lax
from jax.experimental import pallas as pl
from jax.experimental.pallas import tpu as pltpu
from jax.sharding import PartitionSpec as P

MESH = pl.DeviceIdType.MESH
F32, BF16 = jnp.float32, jnp.bfloat16
NY, NX, NZ = 4, 2, 8
NO = NY * NX
CAP = 10
TR = 16
TILES = NZ * CAP // TR
BR = NO * TR
DISP = (0, -1, 1, -2, 2, -3, 3, 4)
SPANS = tuple(
    tuple(sorted({(TR * t + i) // CAP for i in range(TR)})) for t in range(TILES)
)
FAR_TO_NEAR = ((7, 6, 4, 2), (7, 5, 3, 1))
LC = 256


def dot(a, b, ca=1, cb=0):
    return lax.dot_general(a, b, (((ca,), (cb,)), ((), ())), preferred_element_type=F32)


def kernel(
    x_ref, c_ref, info_ref, up_ref, down_ref,
    gx_ref, gs_ref, gu_ref, gd_ref,
    xa, ca, ma, smat, gmat, sx, rx, puf, own, ps, pr, qs, qr, ag, dxs, dxr,
    r0o, r0i, rso, rsi, sco, sci, tf,
    ag_s, ag_r, yx_s, yx_r, dp_s, dp_r, rt_s, rt_r, rs_s, rs_r, sc_s, sc_r,
):
    tok, dl = x_ref.shape
    hid = up_ref.shape[1]
    half_rows = BR // 2
    half_lanes = dl // 2
    me = lax.axis_index("ep")
    dp = lax.axis_index("dp")
    z, yx = me % NZ, me // NZ
    y, x = yx // NX, yx % NX
    core, hi = dp % 2, dp // 2
    neighbour = (yx * NZ + (z + 1) % NZ, yx * NZ + (z + NZ - 1) % NZ)
    core_peer, hi_peer = hi * 2 + (1 - core), (1 - hi) * 2 + core

    def at_offset(o, sign):
        dy, dx = o // NX, o % NX
        there = ((y + sign * dy + NY) % NY) * NX + (x + sign * dx + NX) % NX
        return there * NZ + z

    def remote(src, dst, ss, rs, device):
        return pltpu.make_async_remote_copy(
            src_ref=src, dst_ref=dst, send_sem=ss, recv_sem=rs, device_id=device, device_id_type=MESH
        )

    barrier = pltpu.get_barrier_semaphore()
    peers = [{"ep": n} for n in neighbour]
    peers += [{"ep": at_offset(o, 1)} for o in range(1, NO)]
    peers += [{"dp": core_peer}, {"dp": hi_peer}]
    for peer in peers:
        pl.semaphore_signal(barrier, inc=1, device_id=peer, device_id_type=MESH)

    info = info_ref[...]
    ids = [info[k : k + 1, :] for k in range(2)]
    expert_no = lax.broadcasted_iota(jnp.int32, (NO * NZ // 2, tok), 0).astype(F32)
    hot = [jnp.where(expert_no == ids[k], 1.0, 0.0) for k in range(2)]
    earlier = lax.broadcasted_iota(jnp.int32, (tok, tok), 0) < lax.broadcasted_iota(
        jnp.int32, (tok, tok), 1
    )
    before = dot((hot[0] + hot[1]).astype(BF16), jnp.where(earlier, 1.0, 0.0).astype(BF16))
    code = [
        ids[k] * 16.0 + jnp.sum(before * hot[k], axis=0, keepdims=True) for k in range(2)
    ]
    line = lax.broadcasted_iota(jnp.int32, (8, tok), 0)
    ma[0:8, :] = jnp.where(line == 0, code[0], jnp.where(line == 1, code[1], info))
    pl.semaphore_wait(barrier, len(peers))

    def block(ref, own_ref, j):
        return own_ref if j == 0 else ref.at[(j - 1) * tok : j * tok, :]

    def gather_sent(way, step, n):
        return step < 3 or n == way or (way == 0 and n == 2)

    def gather_copy(way, step, n):
        src = 0 if step == 0 else 2 * step - 1 + way
        dst = 7 if step == 3 else 2 * step + 1 + way
        if n == 2:
            a, b = ma.at[src * 8 : src * 8 + 8, :], ma.at[dst * 8 : dst * 8 + 8, :]
        else:
            ref, own_ref = ((xa, x_ref), (ca, c_ref))[n]
            a, b = block(ref, own_ref, src), block(ref, own_ref, dst)
        sem = (way * 4 + step) * 3 + n
        return remote(a, b, ag_s.at[sem], ag_r.at[sem], {"ep": neighbour[way]})

    def gather_start(step):
        for n in range(3):
            for way in range(2):
                gather_copy(way, step, n).start()

    def gather_next(step):
        for n in range(3):
            for way in range(2):
                if gather_sent(way, step, n):
                    gather_copy(way, step, n).wait_recv()
                if step < 3 and gather_sent(way, step + 1, n):
                    gather_copy(way, step + 1, n).start()

    rho = lax.broadcasted_iota(jnp.int32, (BR, tok), 0)
    o_of = rho >> 4
    i_of = rho & 15
    to_yx = ((y + (o_of >> 1)) & (NY - 1)) * NX + ((x + (o_of & 1)) & (NX - 1))
    expert_of = to_yx * (NZ // 2) + z // 2

    def matches(t, j):
        rank = i_of + (TR * t - CAP * j)
        good = jnp.logical_and(rank >= 0, rank < CAP)
        want = jnp.where(good, expert_of * 16 + rank, -1).astype(F32)
        return [want == ma[j * 8 + k : j * 8 + k + 1, :] for k in range(2)]

    def rows_of(t):
        return pl.ds(t * BR, BR)

    def yx_copy(t, o):
        rows = pl.ds(t * BR + o * TR, TR)
        return remote(sx.at[rows, :], rx.at[rows, :], yx_s.at[t], yx_r.at[t], {"ep": at_offset(o, 1)})

    def yx_all(t):
        rows = pl.ds(t * BR + TR, BR - TR)
        return remote(sx.at[rows, :], rx.at[rows, :], yx_s.at[t], yx_r.at[t], {"ep": at_offset(1, 1)})

    def select(t):
        for n, j in enumerate(SPANS[t]):
            first, second = matches(t, j)
            lanes = pl.ds(n * tok, tok)
            smat[rows_of(t), lanes] = jnp.where(jnp.logical_or(first, second), 1.0, 0.0).astype(BF16)
            gates = [ma[j * 8 + 2 + k : j * 8 + 3 + k, :] for k in range(2)]
            gmat[:, lanes] = jnp.where(first, gates[0], jnp.where(second, gates[1], 0.0)).astype(BF16)

        def part(i, carry):
            lanes = pl.ds(pl.multiple_of(i * LC, LC), LC)
            later = pl.ds(pl.multiple_of(dl + i * LC, LC), LC)
            for pick, ref, own_ref, out in ((smat, xa, x_ref, lanes), (gmat, ca, c_ref, later)):
                total = None
                for n, j in enumerate(SPANS[t]):
                    chosen = pick[rows_of(t) if pick is smat else slice(0, BR), n * tok : (n + 1) * tok]
                    one = dot(chosen, block(ref, own_ref, j)[:, lanes])
                    total = one if total is None else total + one
                sx[rows_of(t), out] = total.astype(BF16)
            return carry

        lax.fori_loop(0, dl // LC, part, 0)
        for o in range(1, NO):
            yx_copy(t, o).start()
        rx[t * BR : t * BR + TR, :] = sx[t * BR : t * BR + TR, :]

    def dp_copy(t, stage):
        sems = (dp_s.at[t * 3 + stage], dp_r.at[t * 3 + stage])
        here = pl.ds(t * half_rows, half_rows)
        if stage == 0:
            return remote(ps.at[here, :], pr.at[here, :], *sems, {"dp": core_peer})
        if stage == 1:
            return remote(qs.at[here, :], qr.at[here, :], *sems, {"dp": hi_peer})
        mine = pl.ds(pl.multiple_of(t * BR + core * half_rows, half_rows), half_rows)
        return remote(ag.at[mine, :], ag.at[mine, :], *sems, {"dp": core_peer})

    def hidden(t):
        yx_all(t).wait_recv()

        def part(i, carry):
            cols = pl.ds(pl.multiple_of(i * LC, LC), LC)
            later = pl.ds(pl.multiple_of(hid + i * LC, LC), LC)
            puf[:, cols] = dot(rx[rows_of(t), 0:dl], up_ref[:, cols])
            puf[:, later] = dot(rx[rows_of(t), dl : 2 * dl], down_ref[cols, :], 1, 1)
            return carry

        lax.fori_loop(0, hid // LC, part, 0)
        here = pl.ds(t * half_rows, half_rows)
        theirs = pl.ds(pl.multiple_of((1 - core) * half_rows, half_rows), half_rows)
        mine = pl.ds(pl.multiple_of(core * half_rows, half_rows), half_rows)
        ps[here, :] = puf[theirs, :].astype(BF16)
        dp_copy(t, 0).start()
        own[here, :] = puf[mine, :]

    def chip_sum(t):
        dp_copy(t, 0).wait_recv()
        here = pl.ds(t * half_rows, half_rows)
        qs[here, :] = (own[here, :] + pr[here, :].astype(F32)).astype(BF16)
        dp_copy(t, 1).start()

    def activate(t):
        dp_copy(t, 1).wait_recv()
        here = pl.ds(t * half_rows, half_rows)
        mine = pl.ds(pl.multiple_of(t * BR + core * half_rows, half_rows), half_rows)
        preact = qs[here, 0:hid].astype(F32) + qr[here, 0:hid].astype(F32)
        upstream = qs[here, hid : 2 * hid].astype(F32) + qr[here, hid : 2 * hid].astype(F32)
        sig = 1.0 / (1.0 + jnp.exp(-preact))
        act = (preact * sig).astype(BF16)
        ag[mine, 0:hid] = act
        ag[mine, hid : 2 * hid] = (upstream * (sig * (1.0 + preact * (1.0 - sig)))).astype(BF16)
        score = jnp.sum(act.astype(F32) * upstream, axis=1, keepdims=True)
        ag[mine, 2 * hid : 2 * hid + 128] = jnp.broadcast_to(score, (half_rows, 128)).astype(BF16)
        dp_copy(t, 2).start()

    def back_copy(t, o):
        rows = pl.ds(t * BR + o * TR, TR)
        return remote(dxs.at[rows, :], dxr.at[rows, :], rt_s.at[t], rt_r.at[t], {"ep": at_offset(o, -1)})

    def back_all(t):
        rows = pl.ds(t * BR + TR, BR - TR)
        return remote(dxs.at[rows, :], dxr.at[rows, :], rt_s.at[t], rt_r.at[t], {"ep": at_offset(1, -1)})

    def send_back(t):
        dp_copy(t, 2).wait_recv()

        def part(i, carry):
            cols = pl.ds(pl.multiple_of(i * LC, LC), LC)
            dxs[rows_of(t), cols] = dot(ag[rows_of(t), hid : 2 * hid], up_ref[cols, :], 1, 1).astype(BF16)
            return carry

        lax.fori_loop(0, dl // LC, part, 0)
        dxs[rows_of(t), dl : dl + 128] = ag[rows_of(t), 2 * hid : 2 * hid + 128]
        for o in range(1, NO):
            back_copy(t, o).start()
        dxr[t * BR : t * BR + TR, :] = dxs[t * BR : t * BR + TR, :]

    def token_sum(j, lo, hi_lane):
        total = None
        for t in range(TILES):
            if j in SPANS[t]:
                n = SPANS[t].index(j)
                one = dot(smat[rows_of(t), n * tok : (n + 1) * tok], dxr[rows_of(t), lo:hi_lane], 0, 0)
                total = one if total is None else total + one
        return total

    def score_sum(j):
        sums = [0.0, 0.0]
        for t in range(TILES):
            if j in SPANS[t]:
                value = dxr[rows_of(t), dl : dl + 128].astype(F32)
                for k, hit in enumerate(matches(t, j)):
                    sums[k] = sums[k] + jnp.sum(jnp.where(hit, value, 0.0), axis=0, keepdims=True)
        return jnp.where(line == 0, sums[0], jnp.where(line == 1, sums[1], 0.0))

    def sum_copy(way, step):
        n = way * 4 + step
        sems = (rs_s.at[n], rs_r.at[n])
        if step == 0:
            rows = pl.ds(way * tok, tok)
            return remote(r0o.at[rows, :], r0i.at[rows, :], *sems, {"ep": neighbour[way]})
        rows = pl.ds((way * 3 + step - 1) * tok, tok)
        return remote(rso.at[rows, :], rsi.at[rows, :], *sems, {"ep": neighbour[way]})

    def score_copy(way, step):
        n = way * 4 + step
        rows = pl.ds(n * 8, 8)
        return remote(sco.at[rows, :], sci.at[rows, :], sc_s.at[n], sc_r.at[n], {"ep": neighbour[way]})

    def scored(way, step):
        return step > 0 or way == 0

    def sum_first():
        for way in range(2):
            lo = way * half_lanes
            r0o[way * tok : (way + 1) * tok, :] = token_sum(7, lo, lo + half_lanes).astype(BF16)
            sum_copy(way, 0).start()
        sco[0:8, :] = score_sum(7)
        score_copy(0, 0).start()

    def sum_ready(way, step):
        j = FAR_TO_NEAR[way][step]
        for lo in (0, half_lanes):
            tf[way * tok : (way + 1) * tok, lo : lo + half_lanes] = token_sum(j, lo, lo + half_lanes)
        n = way * 4 + step
        sco[n * 8 : n * 8 + 8, :] = score_sum(j)

    def sum_next(way, step):
        mine = slice(way * tok, (way + 1) * tok)
        out = slice((way * 3 + step - 1) * tok, (way * 3 + step) * tok)
        sum_copy(way, step - 1).wait_recv()
        if step == 1:
            lo = way * half_lanes
            other = half_lanes - lo
            rso[out, lo : lo + half_lanes] = (
                tf[mine, lo : lo + half_lanes] + r0i[mine, :].astype(F32)
            ).astype(BF16)
            rso[out, other : other + half_lanes] = tf[mine, other : other + half_lanes].astype(BF16)
        else:
            came = slice((way * 3 + step - 2) * tok, (way * 3 + step - 1) * tok)
            rso[out, :] = (tf[mine, :] + rsi[came, :].astype(F32)).astype(BF16)
        sum_copy(way, step).start()
        n = way * 4 + step
        if scored(way, step - 1):
            score_copy(way, step - 1).wait_recv()
            sco[n * 8 : n * 8 + 8, :] += sci[n * 8 - 8 : n * 8, :]
        score_copy(way, step).start()

    def up_gradient():
        def part(i, carry):
            cols = pl.ds(pl.multiple_of(i * LC, LC), LC)
            gu_ref[cols, :] = dot(rx[:, cols], ag[:, hid : 2 * hid], 0, 0).astype(BF16)
            return carry

        lax.fori_loop(0, dl // LC, part, 0)

    def down_gradient():
        def part(i, carry):
            cols = pl.ds(pl.multiple_of(i * LC, LC), LC)
            later = pl.ds(pl.multiple_of(dl + i * LC, LC), LC)
            gd_ref[:, cols] = dot(ag[:, 0:hid], rx[:, later], 0, 0).astype(BF16)
            return carry

        lax.fori_loop(0, dl // LC, part, 0)

    gather_start(0)
    gather_next(0)
    select(0)
    gather_next(1)
    select(1)
    select(2)
    hidden(0)
    chip_sum(0)
    activate(0)
    send_back(0)
    gather_next(2)
    select(3)
    hidden(1)
    hidden(2)
    chip_sum(1)
    chip_sum(2)
    gather_next(3)
    select(4)
    activate(1)
    activate(2)
    hidden(3)
    send_back(1)
    chip_sum(3)
    send_back(2)
    activate(3)
    hidden(4)
    chip_sum(4)
    send_back(3)
    activate(4)
    send_back(4)
    for t in range(TILES):
        back_all(t).wait_recv()
    sum_first()
    for step in range(1, 4):
        for way in range(2):
            sum_ready(way, step)
        for way in range(2):
            sum_next(way, step)
        if step == 1:
            up_gradient()
        if step == 2:
            down_gradient()
    for lo in (0, half_lanes):
        tf[0:tok, lo : lo + half_lanes] = token_sum(0, lo, lo + half_lanes)
    scores = score_sum(0)
    for way in range(2):
        sum_copy(way, 3).wait_recv()
        score_copy(way, 3).wait_recv()
    gx_ref[...] = (
        tf[0:tok, :] + rsi[2 * tok : 3 * tok, :].astype(F32) + rsi[5 * tok : 6 * tok, :].astype(F32)
    ).astype(BF16)
    gates = jnp.where(line == 0, ma[2:3, :], jnp.where(line == 1, ma[3:4, :], 1.0))
    gs_ref[...] = (scores + sci[24:32, :] + sci[56:64, :]) / gates

    for way in range(2):
        for step in range(4):
            for n in range(3):
                if gather_sent(way, step, n):
                    gather_copy(way, step, n).wait_send()
            sum_copy(way, step).wait_send()
            if scored(way, step):
                score_copy(way, step).wait_send()
    for t in range(TILES):
        yx_all(t).wait_send()
        back_all(t).wait_send()
        for stage in range(3):
            dp_copy(t, stage).wait_send()


def on_device(tokens, cotangent, gate_prob, expert_ids, w_up, w_down):
    tok, dl = tokens.shape
    hid = w_up.shape[2]
    info = jnp.concatenate(
        [expert_ids.astype(F32), gate_prob.astype(F32), jnp.zeros((tok, 4), F32)], axis=1
    ).T
    vmem = pl.BlockSpec(memory_space=pltpu.VMEM)
    rows = TILES * BR
    halves = rows // 2
    wide = max(len(s) for s in SPANS) * tok
    scratch = [
        pltpu.VMEM((7 * tok, dl), BF16),
        pltpu.VMEM((7 * tok, dl), BF16),
        pltpu.VMEM((8 * 8, tok), F32),
        pltpu.VMEM((rows, wide), BF16),
        pltpu.VMEM((BR, wide), BF16),
        pltpu.VMEM((rows, 2 * dl), BF16),
        pltpu.VMEM((rows, 2 * dl), BF16),
        pltpu.VMEM((BR, 2 * hid), F32),
        pltpu.VMEM((halves, 2 * hid), F32),
        pltpu.VMEM((halves, 2 * hid), BF16),
        pltpu.VMEM((halves, 2 * hid), BF16),
        pltpu.VMEM((halves, 2 * hid), BF16),
        pltpu.VMEM((halves, 2 * hid), BF16),
        pltpu.VMEM((rows, 2 * hid + 128), BF16),
        pltpu.VMEM((rows, dl + 128), BF16),
        pltpu.VMEM((rows, dl + 128), BF16),
        pltpu.VMEM((2 * tok, dl // 2), BF16),
        pltpu.VMEM((2 * tok, dl // 2), BF16),
        pltpu.VMEM((6 * tok, dl), BF16),
        pltpu.VMEM((6 * tok, dl), BF16),
        pltpu.VMEM((8 * 8, tok), F32),
        pltpu.VMEM((8 * 8, tok), F32),
        pltpu.VMEM((2 * tok, dl), F32),
    ]
    for count in (24, TILES, 3 * TILES, TILES, 8, 8):
        scratch += [pltpu.SemaphoreType.DMA((count,))] * 2
    grad_tokens, scores, grad_up, grad_down = pl.pallas_call(
        kernel,
        out_shape=(
            jax.ShapeDtypeStruct((tok, dl), BF16),
            jax.ShapeDtypeStruct((8, tok), F32),
            jax.ShapeDtypeStruct((dl, hid), BF16),
            jax.ShapeDtypeStruct((hid, dl), BF16),
        ),
        in_specs=[vmem] * 5,
        out_specs=(vmem,) * 4,
        scratch_shapes=scratch,
        compiler_params=pltpu.CompilerParams(
            collective_id=0, has_side_effects=True, vmem_limit_bytes=60 * 2**20
        ),
    )(tokens, cotangent, info, w_up[0], w_down[0])
    return grad_tokens, scores[:2].T, grad_up[None], grad_down[None]


def solution(mesh):
    in_specs = (
        P("ep", "dp"),
        P("ep", "dp"),
        P("ep", None),
        P("ep", None),
        P("ep", "dp", None),
        P("ep", None, "dp"),
    )
    out_specs = (P("ep", "dp"), P("ep", None), P("ep", "dp", None), P("ep", None, "dp"))
    return jax.shard_map(
        on_device, mesh=mesh, in_specs=in_specs, out_specs=out_specs, check_vma=False
    )
```

```python
import functools

import jax
import jax.numpy as jnp
from jax import lax
from jax.experimental import pallas as pl
from jax.experimental.pallas import tpu as pltpu
from jax.sharding import PartitionSpec as P

MESH = pl.DeviceIdType.MESH
F32, BF16 = jnp.float32, jnp.bfloat16
NY, NX, NZ = 4, 2, 8
NO = NY * NX
CAP = 10
TR = 16
TILES = NZ * CAP // TR
BR = NO * TR
DISP = (0, -1, 1, -2, 2, -3, 3, 4)
SPANS = tuple(
    tuple(sorted({(TR * t + i) // CAP for i in range(TR)})) for t in range(TILES)
)
FAR_TO_NEAR = ((7, 6, 4, 2), (7, 5, 3, 1))
LC = 256


def dot(a, b, ca=1, cb=0):
    return lax.dot_general(a, b, (((ca,), (cb,)), ((), ())), preferred_element_type=F32)


def kernel(
    x_ref, c_ref, gate_ref, ids_ref, up_hbm, down_hbm,
    gx_ref, gs_ref, gu_hbm, gd_hbm,
    xa, ca, ma, smat, gmat, sx, rx, puf, own, ps, pr, qs, qr, ag, dxs, dxr,
    rso, rsi, sco, sci, tf, up_ref, down_ref, gu_ref, gd_ref, w_s,
    ag_s, ag_r, yx_s, yx_r, dp_s, dp_r, rt_s, rt_r, rs_s, rs_r, sc_s, sc_r,
):
    tok, dl = x_ref.shape
    hid = up_ref.shape[1]
    slots = TILES * BR
    half_rows = BR // 2
    half_lanes = dl // 2
    me = lax.axis_index("ep")
    dp = lax.axis_index("dp")
    z, yx = me % NZ, me // NZ
    y, x = yx // NX, yx % NX
    core, hi = dp % 2, dp // 2
    neighbour = (yx * NZ + (z + 1) % NZ, yx * NZ + (z + NZ - 1) % NZ)
    core_peer, hi_peer = hi * 2 + (1 - core), (1 - hi) * 2 + core

    def at_offset(o, sign):
        dy, dx = o // NX, o % NX
        there = ((y + sign * dy + NY) % NY) * NX + (x + sign * dx + NX) % NX
        return there * NZ + z

    def remote(src, dst, ss, rs, device):
        return pltpu.make_async_remote_copy(
            src_ref=src, dst_ref=dst, send_sem=ss, recv_sem=rs, device_id=device, device_id_type=MESH
        )

    barrier = pltpu.get_barrier_semaphore()
    peers = [{"ep": n} for n in neighbour]
    peers += [{"ep": at_offset(o, 1)} for o in range(1, NO)]
    peers += [{"dp": core_peer}, {"dp": hi_peer}]
    for peer in peers:
        pl.semaphore_signal(barrier, inc=1, device_id=peer, device_id_type=MESH)

    loads = [
        pltpu.make_async_copy(up_hbm, up_ref, w_s.at[0]),
        pltpu.make_async_copy(down_hbm, down_ref, w_s.at[1]),
    ]
    for load in loads:
        load.start()

    eye = jnp.where(
        lax.broadcasted_iota(jnp.int32, (tok, tok), 0) == lax.broadcasted_iota(jnp.int32, (tok, tok), 1), 1.0, 0.0
    ).astype(BF16)
    ids_rows = dot(ids_ref[...].astype(F32).astype(BF16), eye, 0, 0)
    gate_rows = dot(gate_ref[...], eye, 0, 0)
    ids = [ids_rows[k : k + 1, :] for k in range(2)]
    expert_no = lax.broadcasted_iota(jnp.int32, (NO * NZ // 2, tok), 0).astype(F32)
    hot = [jnp.where(expert_no == ids[k], 1.0, 0.0) for k in range(2)]
    earlier = lax.broadcasted_iota(jnp.int32, (tok, tok), 0) < lax.broadcasted_iota(
        jnp.int32, (tok, tok), 1
    )
    before = dot((hot[0] + hot[1]).astype(BF16), jnp.where(earlier, 1.0, 0.0).astype(BF16))
    code = [
        ids[k] * 16.0 + jnp.sum(before * hot[k], axis=0, keepdims=True) for k in range(2)
    ]
    line = lax.broadcasted_iota(jnp.int32, (8, tok), 0)
    upper = jnp.where(line == 0, code[0], code[1])
    ma[0:8, :] = jnp.where(line < 2, upper, jnp.where(line == 2, gate_rows[0:1, :], gate_rows[1:2, :]))
    pl.semaphore_wait(barrier, len(peers))

    def block(ref, own_ref, j):
        return own_ref if j == 0 else ref.at[(j - 1) * tok : j * tok, :]

    def gather_sent(way, step, n):
        return step < 3 or n == way or (way == 0 and n == 2)

    def gather_copy(way, step, n):
        src = 0 if step == 0 else 2 * step - 1 + way
        dst = 7 if step == 3 else 2 * step + 1 + way
        if n == 2:
            a, b = ma.at[src * 8 : src * 8 + 8, :], ma.at[dst * 8 : dst * 8 + 8, :]
        else:
            ref, own_ref = ((xa, x_ref), (ca, c_ref))[n]
            a, b = block(ref, own_ref, src), block(ref, own_ref, dst)
        sem = (way * 4 + step) * 3 + n
        return remote(a, b, ag_s.at[sem], ag_r.at[sem], {"ep": neighbour[way]})

    def gather_start():
        for n in (2, 0, 1):
            for way in range(2):
                gather_copy(way, 0, n).start()

    def gather_next(step, part):
        for n in ((2, 0), (1,))[part]:
            for way in range(2):
                if gather_sent(way, step, n):
                    gather_copy(way, step, n).wait_recv()
                if step < 3 and gather_sent(way, step + 1, n):
                    gather_copy(way, step + 1, n).start()

    rho = lax.broadcasted_iota(jnp.int32, (BR, tok), 0)
    o_of = rho >> 4
    i_of = rho & 15
    to_yx = ((y + (o_of >> 1)) & (NY - 1)) * NX + ((x + (o_of & 1)) & (NX - 1))
    expert_of = to_yx * (NZ // 2) + z // 2

    def matches(t, j):
        rank = i_of + (TR * t - CAP * j)
        good = jnp.logical_and(rank >= 0, rank < CAP)
        want = jnp.where(good, expert_of * 16 + rank, -1).astype(F32)
        return [want == ma[j * 8 + k : j * 8 + k + 1, :] for k in range(2)]

    def rows_of(t):
        return pl.ds(t * BR, BR)

    def yx_copy(t, part, first, count, o):
        rows = pl.ds(part * slots + t * BR + first, count)
        n = 2 * t + part
        return remote(sx.at[rows, :], rx.at[rows, :], yx_s.at[n], yx_r.at[n], {"ep": at_offset(o, 1)})

    def yx_all(t, part):
        return yx_copy(t, part, TR, BR - TR, 1)

    def select(t, part):
        for n, j in enumerate(SPANS[t]):
            first, second = matches(t, j)
            lanes = pl.ds(n * tok, tok)
            if part == 0:
                smat[rows_of(t), lanes] = jnp.where(jnp.logical_or(first, second), 1.0, 0.0).astype(BF16)
            else:
                gates = [ma[j * 8 + 2 + k : j * 8 + 3 + k, :] for k in range(2)]
                gmat[:, lanes] = jnp.where(first, gates[0], jnp.where(second, gates[1], 0.0)).astype(BF16)
        base = part * slots + t * BR

        def piece(i, carry):
            lanes = pl.ds(pl.multiple_of(i * LC, LC), LC)
            total = None
            for n, j in enumerate(SPANS[t]):
                if part == 0:
                    one = dot(smat[rows_of(t), n * tok : (n + 1) * tok], block(xa, x_ref, j)[:, lanes])
                else:
                    one = dot(gmat[:, n * tok : (n + 1) * tok], block(ca, c_ref, j)[:, lanes])
                total = one if total is None else total + one
            sx[pl.ds(base, BR), lanes] = total.astype(BF16)
            return carry

        lax.fori_loop(0, dl // LC, piece, 0)
        for o in range(1, NO):
            yx_copy(t, part, o * TR, TR, o).start()
        rx[base : base + TR, :] = sx[base : base + TR, :]

    def dp_copy(t, stage):
        sems = (dp_s.at[t * 3 + stage], dp_r.at[t * 3 + stage])
        here = pl.ds(t * half_rows, half_rows)
        if stage == 0:
            return remote(ps.at[here, :], pr.at[here, :], *sems, {"dp": core_peer})
        if stage == 1:
            return remote(qs.at[here, :], qr.at[here, :], *sems, {"dp": hi_peer})
        mine = pl.ds(pl.multiple_of(t * BR + core * half_rows, half_rows), half_rows)
        return remote(ag.at[mine, :], ag.at[mine, :], *sems, {"dp": core_peer})

    def hidden(t):
        yx_all(t, 0).wait_recv()
        yx_all(t, 1).wait_recv()

        def part(i, carry):
            cols = pl.ds(pl.multiple_of(i * LC, LC), LC)
            later = pl.ds(pl.multiple_of(hid + i * LC, LC), LC)
            puf[:, cols] = dot(rx[rows_of(t), :], up_ref[:, cols])
            puf[:, later] = dot(rx[pl.ds(slots + t * BR, BR), :], down_ref[cols, :], 1, 1)
            return carry

        lax.fori_loop(0, hid // LC, part, 0)
        here = pl.ds(t * half_rows, half_rows)
        theirs = pl.ds(pl.multiple_of((1 - core) * half_rows, half_rows), half_rows)
        mine = pl.ds(pl.multiple_of(core * half_rows, half_rows), half_rows)
        ps[here, :] = puf[theirs, :].astype(BF16)
        dp_copy(t, 0).start()
        own[here, :] = puf[mine, :]

    def chip_sum(t):
        dp_copy(t, 0).wait_recv()
        here = pl.ds(t * half_rows, half_rows)
        qs[here, :] = (own[here, :] + pr[here, :].astype(F32)).astype(BF16)
        dp_copy(t, 1).start()

    def activate(t):
        dp_copy(t, 1).wait_recv()
        here = pl.ds(t * half_rows, half_rows)
        mine = pl.ds(pl.multiple_of(t * BR + core * half_rows, half_rows), half_rows)
        preact = qs[here, 0:hid].astype(F32) + qr[here, 0:hid].astype(F32)
        upstream = qs[here, hid : 2 * hid].astype(F32) + qr[here, hid : 2 * hid].astype(F32)
        sig = 1.0 / (1.0 + jnp.exp(-preact))
        act = (preact * sig).astype(BF16)
        ag[mine, 0:hid] = act
        ag[mine, hid : 2 * hid] = (upstream * (sig * (1.0 + preact * (1.0 - sig)))).astype(BF16)
        score = jnp.sum(act.astype(F32) * upstream, axis=1, keepdims=True)
        ag[mine, 2 * hid : 2 * hid + 128] = jnp.broadcast_to(score, (half_rows, 128)).astype(BF16)
        dp_copy(t, 2).start()

    def back_copy(t, o):
        rows = pl.ds(t * BR + o * TR, TR)
        return remote(dxs.at[rows, :], dxr.at[rows, :], rt_s.at[t], rt_r.at[t], {"ep": at_offset(o, -1)})

    def back_all(t):
        rows = pl.ds(t * BR + TR, BR - TR)
        return remote(dxs.at[rows, :], dxr.at[rows, :], rt_s.at[t], rt_r.at[t], {"ep": at_offset(1, -1)})

    def back_rows(t):
        dp_copy(t, 2).wait_recv()

        def part(i, carry):
            cols = pl.ds(pl.multiple_of(i * LC, LC), LC)
            dxs[rows_of(t), cols] = dot(ag[rows_of(t), hid : 2 * hid], up_ref[cols, :], 1, 1).astype(BF16)
            return carry

        lax.fori_loop(0, dl // LC, part, 0)
        dxs[rows_of(t), dl : dl + 128] = ag[rows_of(t), 2 * hid : 2 * hid + 128]

    def send_back(t):
        for o in range(1, NO):
            back_copy(t, o).start()
        dxr[t * BR : t * BR + TR, :] = dxs[t * BR : t * BR + TR, :]

    def token_sum(j, lo, hi_lane):
        total = None
        for t in range(TILES):
            if j in SPANS[t]:
                n = SPANS[t].index(j)
                one = dot(smat[rows_of(t), n * tok : (n + 1) * tok], dxr[rows_of(t), lo:hi_lane], 0, 0)
                total = one if total is None else total + one
        return total

    def score_sum(j):
        sums = [0.0, 0.0]
        for t in range(TILES):
            if j in SPANS[t]:
                value = dxr[rows_of(t), dl : dl + 128].astype(F32)
                for k, hit in enumerate(matches(t, j)):
                    sums[k] = sums[k] + jnp.sum(jnp.where(hit, value, 0.0), axis=0, keepdims=True)
        return jnp.where(line == 0, sums[0], jnp.where(line == 1, sums[1], 0.0))

    def lanes_of(way, m):
        return half_lanes if (way + m) % 2 else 0

    def sum_rows(way, m):
        return slice((way * 7 + m) * tok, (way * 7 + m + 1) * tok)

    def sum_copy(way, m):
        n = way * 7 + m
        rows = pl.ds(n * tok, tok)
        return remote(rso.at[rows, :], rsi.at[rows, :], rs_s.at[n], rs_r.at[n], {"ep": neighbour[way]})

    def score_copy(way, step):
        n = way * 4 + step
        rows = pl.ds(n * 8, 8)
        return remote(sco.at[rows, :], sci.at[rows, :], sc_s.at[n], sc_r.at[n], {"ep": neighbour[way]})

    def scored(way, step):
        return step > 0 or way == 0

    def sum_ready(way, m):
        lo = lanes_of(way, m)
        tf[way * tok : (way + 1) * tok, :] = token_sum(FAR_TO_NEAR[way][(m + 1) // 2], lo, lo + half_lanes)

    def sum_next(way, m):
        total = tf[way * tok : (way + 1) * tok, :]
        if m >= 2:
            sum_copy(way, m - 2).wait_recv()
            total = total + rsi[sum_rows(way, m - 2), :].astype(F32)
        rso[sum_rows(way, m), :] = total.astype(BF16)
        sum_copy(way, m).start()

    def score_next(way, step):
        n = way * 4 + step
        here = score_sum(FAR_TO_NEAR[way][step])
        if step > 0 and scored(way, step - 1):
            score_copy(way, step - 1).wait_recv()
            here = here + sci[n * 8 - 8 : n * 8, :]
        sco[n * 8 : n * 8 + 8, :] = here
        score_copy(way, step).start()

    def up_gradient():
        def part(i, carry):
            cols = pl.ds(pl.multiple_of(i * LC, LC), LC)
            gu_ref[cols, :] = dot(rx[0:slots, cols], ag[:, hid : 2 * hid], 0, 0).astype(BF16)
            return carry

        lax.fori_loop(0, dl // LC, part, 0)

    def down_gradient():
        def part(i, carry):
            cols = pl.ds(pl.multiple_of(i * LC, LC), LC)
            gd_ref[:, cols] = dot(ag[:, 0:hid], rx[slots : 2 * slots, cols], 0, 0).astype(BF16)
            return carry

        lax.fori_loop(0, dl // LC, part, 0)

    gather_start()
    gather_next(0, 0)
    select(0, 0)
    gather_next(0, 1)
    select(0, 1)
    gather_next(1, 0)
    select(1, 0)
    select(2, 0)
    for load in loads:
        load.wait()
    hidden(0)
    chip_sum(0)
    gather_next(1, 1)
    select(1, 1)
    select(2, 1)
    activate(0)
    back_rows(0)
    gather_next(2, 0)
    select(3, 0)
    hidden(1)
    chip_sum(1)
    gather_next(2, 1)
    select(3, 1)
    activate(1)
    hidden(2)
    chip_sum(2)
    gather_next(3, 0)
    select(4, 0)
    gather_next(3, 1)
    select(4, 1)
    back_rows(1)
    activate(2)
    back_rows(2)
    hidden(3)
    chip_sum(3)
    hidden(4)
    chip_sum(4)
    activate(3)
    activate(4)
    back_rows(4)
    send_back(4)
    back_rows(3)
    send_back(3)
    send_back(2)
    send_back(1)
    send_back(0)
    stores = [
        pltpu.make_async_copy(gu_ref, gu_hbm, w_s.at[2]),
        pltpu.make_async_copy(gd_ref, gd_hbm, w_s.at[3]),
    ]
    up_gradient()
    stores[0].start()
    back_all(4).wait_recv()
    for way in range(2):
        sum_ready(way, 0)
        sum_next(way, 0)
    back_all(3).wait_recv()
    for m in range(1, 7):
        if m == 3:
            back_all(2).wait_recv()
            back_all(1).wait_recv()
        if m == 5:
            back_all(0).wait_recv()
        for way in range(2):
            sum_ready(way, m)
            sum_next(way, m)
        if m == 1:
            down_gradient()
            stores[1].start()
        if m % 2 == 0:
            for way in range(2):
                if m == 2 and way == 0:
                    score_next(0, 0)
                score_next(way, m // 2)
    for n, lo in enumerate((0, half_lanes)):
        tf[n * tok : (n + 1) * tok, :] = token_sum(0, lo, lo + half_lanes)
    scores = score_sum(0)
    for m in (5, 6):
        for way in range(2):
            sum_copy(way, m).wait_recv()
    for m in (5, 6):
        lo = lanes_of(0, m)
        n = lo // half_lanes
        gx_ref[:, lo : lo + half_lanes] = (
            tf[n * tok : (n + 1) * tok, :]
            + rsi[sum_rows(0, m), :].astype(F32)
            + rsi[sum_rows(1, 11 - m), :].astype(F32)
        ).astype(BF16)
    for way in range(2):
        score_copy(way, 3).wait_recv()
    gates = jnp.where(line == 0, ma[2:3, :], jnp.where(line == 1, ma[3:4, :], 1.0))
    gs_ref[...] = (scores + sci[24:32, :] + sci[56:64, :]) / gates

    for way in range(2):
        for step in range(4):
            for n in range(3):
                if gather_sent(way, step, n):
                    gather_copy(way, step, n).wait_send()
            if scored(way, step):
                score_copy(way, step).wait_send()
        for m in range(7):
            sum_copy(way, m).wait_send()
    for t in range(TILES):
        for part in range(2):
            yx_all(t, part).wait_send()
        back_all(t).wait_send()
        for stage in range(3):
            dp_copy(t, stage).wait_send()
    for store in stores:
        store.wait()


def on_device(tokens, cotangent, gate_prob, expert_ids, w_up, w_down):
    tok, dl = tokens.shape
    hid = w_up.shape[2]
    vmem = pl.BlockSpec(memory_space=pltpu.VMEM)
    hbm = pl.BlockSpec(memory_space=pl.ANY)
    rows = TILES * BR
    halves = rows // 2
    wide = max(len(s) for s in SPANS) * tok
    scratch = [
        pltpu.VMEM((7 * tok, dl), BF16),
        pltpu.VMEM((7 * tok, dl), BF16),
        pltpu.VMEM((8 * 8, tok), F32),
        pltpu.VMEM((rows, wide), BF16),
        pltpu.VMEM((BR, wide), BF16),
        pltpu.VMEM((2 * rows, dl), BF16),
        pltpu.VMEM((2 * rows, dl), BF16),
        pltpu.VMEM((BR, 2 * hid), F32),
        pltpu.VMEM((halves, 2 * hid), F32),
        pltpu.VMEM((halves, 2 * hid), BF16),
        pltpu.VMEM((halves, 2 * hid), BF16),
        pltpu.VMEM((halves, 2 * hid), BF16),
        pltpu.VMEM((halves, 2 * hid), BF16),
        pltpu.VMEM((rows, 2 * hid + 128), BF16),
        pltpu.VMEM((rows, dl + 128), BF16),
        pltpu.VMEM((rows, dl + 128), BF16),
        pltpu.VMEM((14 * tok, dl // 2), BF16),
        pltpu.VMEM((14 * tok, dl // 2), BF16),
        pltpu.VMEM((8 * 8, tok), F32),
        pltpu.VMEM((8 * 8, tok), F32),
        pltpu.VMEM((2 * tok, dl // 2), F32),
        pltpu.VMEM((dl, hid), BF16),
        pltpu.VMEM((hid, dl), BF16),
        pltpu.VMEM((dl, hid), BF16),
        pltpu.VMEM((hid, dl), BF16),
        pltpu.SemaphoreType.DMA((4,)),
    ]
    for count in (24, 2 * TILES, 3 * TILES, TILES, 14, 8):
        scratch += [pltpu.SemaphoreType.DMA((count,))] * 2
    grad_tokens, scores, grad_up, grad_down = pl.pallas_call(
        kernel,
        out_shape=(
            jax.ShapeDtypeStruct((tok, dl), BF16),
            jax.ShapeDtypeStruct((8, tok), F32),
            jax.ShapeDtypeStruct((dl, hid), BF16),
            jax.ShapeDtypeStruct((hid, dl), BF16),
        ),
        in_specs=[vmem] * 4 + [hbm] * 2,
        out_specs=(vmem, vmem, hbm, hbm),
        scratch_shapes=scratch,
        compiler_params=pltpu.CompilerParams(
            collective_id=0, has_side_effects=True, vmem_limit_bytes=60 * 2**20
        ),
    )(tokens, cotangent, gate_prob, expert_ids, w_up[0], w_down[0])
    return grad_tokens, scores[:2].T, grad_up[None], grad_down[None]


def solution(mesh):
    in_specs = (
        P("ep", "dp"),
        P("ep", "dp"),
        P("ep", None),
        P("ep", None),
        P("ep", "dp", None),
        P("ep", None, "dp"),
    )
    out_specs = (P("ep", "dp"), P("ep", None), P("ep", "dp", None), P("ep", None, "dp"))
    return jax.shard_map(
        on_device, mesh=mesh, in_specs=in_specs, out_specs=out_specs, check_vma=False
    )
```

```python
import functools

import jax
import jax.numpy as jnp
from jax import lax
from jax.experimental import pallas as pl
from jax.experimental.pallas import tpu as pltpu
from jax.sharding import PartitionSpec as P

MESH = pl.DeviceIdType.MESH
F32, BF16 = jnp.float32, jnp.bfloat16
NY, NX, NZ = 4, 2, 8
NO = NY * NX
CAP = 10
TR = 16
TILES = NZ * CAP // TR
BR = NO * TR
LAST = NO * CAP
DISP = (0, -1, 1, -2, 2, -3, 3, 4)
SPANS = tuple(
    tuple(sorted({(TR * t + i) // CAP for i in range(TR)})) for t in range(TILES)
)
FAR_TO_NEAR = ((7, 6, 4, 2), (7, 5, 3, 1))
LC = 256
PIECES = 4


def dot(a, b, ca=1, cb=0):
    return lax.dot_general(a, b, (((ca,), (cb,)), ((), ())), preferred_element_type=F32)


def kernel(
    x_ref, c_ref, gate_ref, ids_ref, up_hbm, down_hbm,
    gx_ref, gs_ref, gu_hbm, gd_hbm,
    xa, ca, ma, smat, gmat, sx, rx, puf, own, ps, pr, qs, qr, ag, dxs, dxr,
    rso, rsi, sco, sci, tf, up_ref, down_ref, gu_ref, gd_ref, lmat, lgate, lout, lin, pm, w_s,
    last_s, last_r,
    ag_s, ag_r, yx_s, yx_r, dp_s, dp_r, rt_s, rt_r, rs_s, rs_r, sc_s, sc_r,
):
    tok, dl = x_ref.shape
    hid = up_ref.shape[1]
    slots = TILES * BR
    half_rows = BR // 2
    half_lanes = dl // 2
    me = lax.axis_index("ep")
    dp = lax.axis_index("dp")
    z, yx = me % NZ, me // NZ
    y, x = yx // NX, yx % NX
    core, hi = dp % 2, dp // 2
    neighbour = (yx * NZ + (z + 1) % NZ, yx * NZ + (z + NZ - 1) % NZ)
    core_peer, hi_peer = hi * 2 + (1 - core), (1 - hi) * 2 + core

    def at_offset(o, sign):
        dy, dx = o // NX, o % NX
        there = ((y + sign * dy + NY) % NY) * NX + (x + sign * dx + NX) % NX
        return there * NZ + z

    def remote(src, dst, ss, rs, device):
        return pltpu.make_async_remote_copy(
            src_ref=src, dst_ref=dst, send_sem=ss, recv_sem=rs, device_id=device, device_id_type=MESH
        )

    barrier = pltpu.get_barrier_semaphore()
    peers = [{"ep": n} for n in neighbour]
    peers += [{"ep": at_offset(o, 1)} for o in range(1, NO)]
    peers += [{"dp": core_peer}, {"dp": hi_peer}]
    for peer in peers:
        pl.semaphore_signal(barrier, inc=1, device_id=peer, device_id_type=MESH)

    loads = [
        pltpu.make_async_copy(up_hbm, up_ref, w_s.at[0]),
        pltpu.make_async_copy(down_hbm, down_ref, w_s.at[1]),
    ]
    for load in loads:
        load.start()

    gate_rows = gate_ref[...].astype(F32)
    ids_rows = ids_ref[...].astype(F32)
    ids = [ids_rows[k : k + 1, :] for k in range(2)]
    expert_no = lax.broadcasted_iota(jnp.int32, (NO * NZ // 2, tok), 0).astype(F32)
    hot = [jnp.where(expert_no == ids[k], 1.0, 0.0) for k in range(2)]
    earlier = lax.broadcasted_iota(jnp.int32, (tok, tok), 0) < lax.broadcasted_iota(
        jnp.int32, (tok, tok), 1
    )
    before = dot((hot[0] + hot[1]).astype(BF16), jnp.where(earlier, 1.0, 0.0).astype(BF16))
    code = [
        ids[k] * 16.0 + jnp.sum(before * hot[k], axis=0, keepdims=True) for k in range(2)
    ]
    line = lax.broadcasted_iota(jnp.int32, (8, tok), 0)
    upper = jnp.where(line == 0, code[0], code[1])
    ma[0:8, :] = jnp.where(line < 2, upper, jnp.where(line == 2, gate_rows[0:1, :], gate_rows[1:2, :]))
    pl.semaphore_wait(barrier, len(peers))

    def block(ref, own_ref, j):
        return own_ref if j == 0 else ref.at[(j - 1) * tok : j * tok, :]

    def gather_sent(way, step, n):
        return step < 3 or (way == 0 and n == 2)

    def gather_copy(way, step, n):
        src = 0 if step == 0 else 2 * step - 1 + way
        dst = 7 if step == 3 else 2 * step + 1 + way
        if n == 2:
            a, b = ma.at[src * 8 : src * 8 + 8, :], ma.at[dst * 8 : dst * 8 + 8, :]
        else:
            ref, own_ref = ((xa, x_ref), (ca, c_ref))[n]
            a, b = block(ref, own_ref, src), block(ref, own_ref, dst)
        sem = (way * 4 + step) * 3 + n
        return remote(a, b, ag_s.at[sem], ag_r.at[sem], {"ep": neighbour[way]})

    def gather_start():
        for n in (2, 0, 1):
            for way in range(2):
                gather_copy(way, 0, n).start()

    def gather_next(step, part):
        for n in ((2, 0), (1,))[part]:
            for way in (part, 1 - part):
                if gather_sent(way, step, n):
                    gather_copy(way, step, n).wait_recv()
                if step < 3 and gather_sent(way, step + 1, n):
                    gather_copy(way, step + 1, n).start()
                if step == 2 and n == way:
                    last_hop(way)

    def last_copy(way, h):
        n = way * 2 + h
        rows, lanes = pl.ds(way * LAST, LAST), pl.ds(h * half_lanes, half_lanes)
        return remote(
            lout.at[rows, lanes], lin.at[rows, lanes], last_s.at[n], last_r.at[n], {"ep": neighbour[way]}
        )

    def last_hop(way):
        j = 5 + way
        spot = lax.broadcasted_iota(jnp.int32, (LAST, tok), 0)
        o_at = (spot * 205) >> 11
        there = ((y + (o_at >> 1)) & (NY - 1)) * NX + ((x + (o_at & 1)) & (NX - 1))
        pair = ((z + (1, NZ - 1)[way]) % NZ) // 2
        want = ((there * (NZ // 2) + pair) * 16 + (spot - o_at * CAP)).astype(F32)
        first, second = [want == ma[j * 8 + k : j * 8 + k + 1, :] for k in range(2)]
        mine = slice(way * LAST, (way + 1) * LAST)
        lmat[mine, :] = jnp.where(jnp.logical_or(first, second), 1.0, 0.0).astype(BF16)
        if way == 1:
            gates = [ma[j * 8 + 2 + k : j * 8 + 3 + k, :] for k in range(2)]
            lgate[...] = jnp.where(first, gates[0], jnp.where(second, gates[1], 0.0)).astype(BF16)
        ref, own_ref = ((xa, x_ref), (ca, c_ref))[way]

        def piece(i, carry):
            lanes = pl.ds(pl.multiple_of(i * 128, 128), 128)
            pick = lmat[mine, :] if way == 0 else lgate[...]
            lout[mine, lanes] = dot(pick, block(ref, own_ref, j)[:, lanes]).astype(BF16)
            return carry

        each = half_lanes // 128
        for h in range(2):
            lax.fori_loop(h * each, (h + 1) * each, piece, 0)
            last_copy(way, h).start()

    rho = lax.broadcasted_iota(jnp.int32, (BR, tok), 0)
    o_of = rho >> 4
    i_of = rho & 15
    to_yx = ((y + (o_of >> 1)) & (NY - 1)) * NX + ((x + (o_of & 1)) & (NX - 1))
    expert_of = to_yx * (NZ // 2) + z // 2

    def matches(t, j):
        rank = i_of + (TR * t - CAP * j)
        good = jnp.logical_and(rank >= 0, rank < CAP)
        want = jnp.where(good, expert_of * 16 + rank, -1).astype(F32)
        return [want == ma[j * 8 + k : j * 8 + k + 1, :] for k in range(2)]

    def rows_of(t):
        return pl.ds(t * BR, BR)

    def yx_copy(t, part, h, first, count, o):
        rows = pl.ds(part * slots + t * BR + first, count)
        lanes = pl.ds(0, dl)
        n = 2 * t + part
        if t == TILES - 1:
            lanes = pl.ds(h * half_lanes, half_lanes)
            n += part + h
        return remote(
            sx.at[rows, lanes], rx.at[rows, lanes], yx_s.at[n], yx_r.at[n], {"ep": at_offset(o, 1)}
        )

    def yx_all(t, part):
        return [yx_copy(t, part, h, TR, BR - TR, 1) for h in range(2 if t == TILES - 1 else 1)]

    def pick_matrices(t, part):
        for n, j in enumerate(SPANS[t]):
            first, second = matches(t, j)
            lanes = pl.ds(n * tok, tok)
            if part == 0:
                smat[rows_of(t), lanes] = jnp.where(jnp.logical_or(first, second), 1.0, 0.0).astype(BF16)
            elif j < 7:
                gates = [ma[j * 8 + 2 + k : j * 8 + 3 + k, :] for k in range(2)]
                gmat[:, lanes] = jnp.where(first, gates[0], jnp.where(second, gates[1], 0.0)).astype(BF16)

    def select(t, part, h=0):
        if h == 0:
            pick_matrices(t, part)
        base = part * slots + t * BR
        last = t == TILES - 1
        width = 128 if last else LC

        def piece(i, carry):
            lanes = pl.ds(pl.multiple_of(i * width, width), width)
            total = None
            for n, j in enumerate(SPANS[t]):
                if j == 7:
                    one = dot(pm[...], lin[part * LAST : (part + 1) * LAST, lanes])
                elif part == 0:
                    one = dot(smat[rows_of(t), n * tok : (n + 1) * tok], block(xa, x_ref, j)[:, lanes])
                else:
                    one = dot(gmat[:, n * tok : (n + 1) * tok], block(ca, c_ref, j)[:, lanes])
                total = one if total is None else total + one
            sx[pl.ds(base, BR), lanes] = total.astype(BF16)
            return carry

        each = half_lanes // 128
        lax.fori_loop(*((h * each, (h + 1) * each) if last else (0, dl // LC)), piece, 0)
        for o in range(1, NO):
            yx_copy(t, part, h, o * TR, TR, o).start()
        span = slice(h * half_lanes, (h + 1) * half_lanes) if last else slice(0, dl)
        rx[base : base + TR, span] = sx[base : base + TR, span]

    def dp_copy(t, stage):
        sems = (dp_s.at[t * 3 + stage], dp_r.at[t * 3 + stage])
        here = pl.ds(t * half_rows, half_rows)
        if stage == 0:
            return remote(ps.at[here, :], pr.at[here, :], *sems, {"dp": core_peer})
        if stage == 1:
            return remote(qs.at[here, :], qr.at[here, :], *sems, {"dp": hi_peer})
        mine = pl.ds(pl.multiple_of(t * BR + core * half_rows, half_rows), half_rows)
        return remote(ag.at[mine, :], ag.at[mine, :], *sems, {"dp": core_peer})

    def hidden(t):
        for half in range(2):
            for copy in yx_all(t, half):
                copy.wait_recv()

        def part(i, carry):
            cols = pl.ds(pl.multiple_of(i * LC, LC), LC)
            later = pl.ds(pl.multiple_of(hid + i * LC, LC), LC)
            puf[:, cols] = dot(rx[rows_of(t), :], up_ref[:, cols])
            puf[:, later] = dot(rx[pl.ds(slots + t * BR, BR), :], down_ref[cols, :], 1, 1)
            return carry

        lax.fori_loop(0, hid // LC, part, 0)
        here = pl.ds(t * half_rows, half_rows)
        theirs = pl.ds(pl.multiple_of((1 - core) * half_rows, half_rows), half_rows)
        mine = pl.ds(pl.multiple_of(core * half_rows, half_rows), half_rows)
        ps[here, :] = puf[theirs, :].astype(BF16)
        dp_copy(t, 0).start()
        own[here, :] = puf[mine, :]

    def chip_sum(t):
        dp_copy(t, 0).wait_recv()
        here = pl.ds(t * half_rows, half_rows)
        qs[here, :] = (own[here, :] + pr[here, :].astype(F32)).astype(BF16)
        dp_copy(t, 1).start()

    def activate(t):
        dp_copy(t, 1).wait_recv()
        here = pl.ds(t * half_rows, half_rows)
        mine = pl.ds(pl.multiple_of(t * BR + core * half_rows, half_rows), half_rows)
        preact = qs[here, 0:hid].astype(F32) + qr[here, 0:hid].astype(F32)
        upstream = qs[here, hid : 2 * hid].astype(F32) + qr[here, hid : 2 * hid].astype(F32)
        sig = 1.0 / (1.0 + jnp.exp(-preact))
        act = (preact * sig).astype(BF16)
        ag[mine, 0:hid] = act
        ag[mine, hid : 2 * hid] = (upstream * (sig * (1.0 + preact * (1.0 - sig)))).astype(BF16)
        score = jnp.sum(act.astype(F32) * upstream, axis=1, keepdims=True)
        ag[mine, 2 * hid : 2 * hid + 128] = jnp.broadcast_to(score, (half_rows, 128)).astype(BF16)
        dp_copy(t, 2).start()

    def back_copy(t, o):
        rows = pl.ds(t * BR + o * TR, TR)
        return remote(dxs.at[rows, :], dxr.at[rows, :], rt_s.at[t], rt_r.at[t], {"ep": at_offset(o, -1)})

    def back_all(t):
        rows = pl.ds(t * BR + TR, BR - TR)
        return remote(dxs.at[rows, :], dxr.at[rows, :], rt_s.at[t], rt_r.at[t], {"ep": at_offset(1, -1)})

    def back_rows(t):
        dp_copy(t, 2).wait_recv()

        def part(i, carry):
            cols = pl.ds(pl.multiple_of(i * LC, LC), LC)
            dxs[rows_of(t), cols] = dot(ag[rows_of(t), hid : 2 * hid], up_ref[cols, :], 1, 1).astype(BF16)
            return carry

        lax.fori_loop(0, dl // LC, part, 0)
        dxs[rows_of(t), dl : dl + 128] = ag[rows_of(t), 2 * hid : 2 * hid + 128]

    def send_back(t):
        for o in range(1, NO):
            back_copy(t, o).start()
        dxr[t * BR : t * BR + TR, :] = dxs[t * BR : t * BR + TR, :]

    def token_sum(j, lo, hi_lane):
        total = None
        for t in range(TILES):
            if j in SPANS[t]:
                n = SPANS[t].index(j)
                one = dot(smat[rows_of(t), n * tok : (n + 1) * tok], dxr[rows_of(t), lo:hi_lane], 0, 0)
                total = one if total is None else total + one
        return total

    def score_sum(j):
        sums = [0.0, 0.0]
        for t in range(TILES):
            if j in SPANS[t]:
                value = dxr[rows_of(t), dl : dl + 128].astype(F32)
                for k, hit in enumerate(matches(t, j)):
                    sums[k] = sums[k] + jnp.sum(jnp.where(hit, value, 0.0), axis=0, keepdims=True)
        return jnp.where(line == 0, sums[0], jnp.where(line == 1, sums[1], 0.0))

    def lanes_of(way, m):
        return half_lanes if (way + m) % 2 else 0

    def sum_rows(way, m):
        return slice((way * 7 + m) * tok, (way * 7 + m + 1) * tok)

    def sum_copy(way, m):
        n = way * 7 + m
        rows = pl.ds(n * tok, tok if m else LAST)
        return remote(rso.at[rows, :], rsi.at[rows, :], rs_s.at[n], rs_r.at[n], {"ep": neighbour[way]})

    def score_copy(way, step):
        n = way * 4 + step
        rows = pl.ds(n * 8, 8)
        return remote(sco.at[rows, :], sci.at[rows, :], sc_s.at[n], sc_r.at[n], {"ep": neighbour[way]})

    def scored(way, step):
        return step > 0 or way == 0

    def sum_ready(way, m):
        lo = lanes_of(way, m)
        if m == 0:
            tf[way * tok : way * tok + LAST, :] = dot(
                pm[...], dxr[rows_of(TILES - 1), lo : lo + half_lanes], 0, 0
            )
            return
        tf[way * tok : (way + 1) * tok, :] = token_sum(FAR_TO_NEAR[way][(m + 1) // 2], lo, lo + half_lanes)

    def sum_next(way, m):
        count = tok if m else LAST
        total = tf[way * tok : way * tok + count, :]
        first = (way * 7 + m) * tok
        if m >= 2:
            sum_copy(way, m - 2).wait_recv()
        if m == 2:
            came = rsi[first - 2 * tok : first - 2 * tok + LAST, :]
            total = total + dot(lmat[(1 - way) * LAST : (2 - way) * LAST, :], came, 0, 0)
        elif m > 2:
            total = total + rsi[sum_rows(way, m - 2), :].astype(F32)
        rso[first : first + count, :] = total.astype(BF16)
        sum_copy(way, m).start()

    def score_next(way, step):
        n = way * 4 + step
        here = score_sum(FAR_TO_NEAR[way][step])
        if step > 0 and scored(way, step - 1):
            score_copy(way, step - 1).wait_recv()
            here = here + sci[n * 8 - 8 : n * 8, :]
        sco[n * 8 : n * 8 + 8, :] = here
        score_copy(way, step).start()

    def up_gradient():
        def part(i, carry):
            cols = pl.ds(pl.multiple_of(i * LC, LC), LC)
            gu_ref[cols, :] = dot(rx[0:slots, cols], ag[:, hid : 2 * hid], 0, 0).astype(BF16)
            return carry

        lax.fori_loop(0, dl // LC, part, 0)

    def down_gradient():
        def part(i, carry):
            cols = pl.ds(pl.multiple_of(i * LC, LC), LC)
            gd_ref[:, cols] = dot(ag[:, 0:hid], rx[slots : 2 * slots, cols], 0, 0).astype(BF16)
            return carry

        lax.fori_loop(0, dl // LC, part, 0)

    gather_start()
    gather_next(0, 0)
    select(0, 0)
    gather_next(0, 1)
    select(0, 1)
    gather_next(1, 0)
    select(1, 0)
    select(2, 0)
    slot_row = lax.broadcasted_iota(jnp.int32, (BR, LAST), 0)
    rank_row = (slot_row & 15) - (TR - CAP)
    spot_of = jnp.where(rank_row >= 0, (slot_row >> 4) * CAP + rank_row, -1)
    pm[...] = jnp.where(spot_of == lax.broadcasted_iota(jnp.int32, (BR, LAST), 1), 1.0, 0.0).astype(BF16)
    for load in loads:
        load.wait()
    hidden(0)
    chip_sum(0)
    gather_next(1, 1)
    select(1, 1)
    select(2, 1)
    activate(0)
    back_rows(0)
    gather_next(2, 0)
    select(3, 0)
    hidden(1)
    chip_sum(1)
    gather_next(2, 1)
    select(3, 1)
    activate(1)
    hidden(2)
    chip_sum(2)
    gather_copy(0, 3, 2).wait_recv()
    for h in range(2):
        for part in range(2):
            last_copy(part, h).wait_recv()
            select(4, part, h)
    back_rows(1)
    activate(2)
    back_rows(2)
    hidden(3)
    chip_sum(3)
    hidden(4)
    chip_sum(4)
    activate(3)
    activate(4)
    back_rows(4)
    send_back(4)
    back_rows(3)
    send_back(3)
    send_back(2)
    send_back(1)
    send_back(0)
    stores = [
        pltpu.make_async_copy(gu_ref, gu_hbm, w_s.at[2]),
        pltpu.make_async_copy(gd_ref, gd_hbm, w_s.at[3]),
    ]
    up_gradient()
    stores[0].start()
    back_all(4).wait_recv()
    for way in range(2):
        sum_ready(way, 0)
        sum_next(way, 0)
    back_all(3).wait_recv()
    for m in range(1, 7):
        if m == 3:
            back_all(2).wait_recv()
            back_all(1).wait_recv()
        if m == 5:
            back_all(0).wait_recv()
        for way in range(2):
            sum_ready(way, m)
            sum_next(way, m)
        if m == 1:
            down_gradient()
            stores[1].start()
        if m % 2 == 0:
            for way in range(2):
                if m == 2 and way == 0:
                    score_next(0, 0)
                score_next(way, m // 2)
    for n, lo in enumerate((0, half_lanes)):
        tf[n * tok : (n + 1) * tok, :] = token_sum(0, lo, lo + half_lanes)
    scores = score_sum(0)
    for m in (5, 6):
        for way in range(2):
            sum_copy(way, m).wait_recv()
    for m in (5, 6):
        lo = lanes_of(0, m)
        n = lo // half_lanes
        gx_ref[:, lo : lo + half_lanes] = (
            tf[n * tok : (n + 1) * tok, :]
            + rsi[sum_rows(0, m), :].astype(F32)
            + rsi[sum_rows(1, 11 - m), :].astype(F32)
        ).astype(BF16)
    for way in range(2):
        score_copy(way, 3).wait_recv()
    gates = jnp.where(line == 0, ma[2:3, :], jnp.where(line == 1, ma[3:4, :], 1.0))
    gs_ref[...] = ((scores + sci[24:32, :] + sci[56:64, :]) / gates)[0:2, :]

    for way in range(2):
        for step in range(4):
            for n in range(3):
                if gather_sent(way, step, n):
                    gather_copy(way, step, n).wait_send()
            if scored(way, step):
                score_copy(way, step).wait_send()
        for m in range(7):
            sum_copy(way, m).wait_send()
        for h in range(2):
            last_copy(way, h).wait_send()
    for t in range(TILES):
        for part in range(2):
            for copy in yx_all(t, part):
                copy.wait_send()
        back_all(t).wait_send()
        for stage in range(3):
            dp_copy(t, stage).wait_send()
    for store in stores:
        store.wait()


def hand_over(*refs):
    sems = refs[12]
    loads, stores = [], []
    for n in range(4):
        pieces = PIECES if refs[n].shape[0] % (16 * PIECES) == 0 else 1
        size = refs[n].shape[0] // pieces
        for i in range(pieces):
            rows = pl.ds(i * size, size)
            held = refs[8 + n].at[rows, :]
            loads.append(pltpu.make_async_copy(refs[n].at[rows, :], held, sems.at[0, n, i]))
            stores.append(pltpu.make_async_copy(held, refs[4 + n].at[rows, :], sems.at[1, n, i]))
    for load in loads:
        load.start()
    for load, store in zip(loads, stores):
        load.wait()
        store.start()
    for store in stores:
        store.wait()


def on_device(tokens, cotangent, gate_prob, expert_ids, w_up, w_down):
    tok, dl = tokens.shape
    hid = w_up.shape[2]
    vmem = pl.BlockSpec(memory_space=pltpu.VMEM)
    hbm = pl.BlockSpec(memory_space=pl.ANY)
    rows = TILES * BR
    halves = rows // 2
    wide = max(len(s) for s in SPANS) * tok
    scratch = [
        pltpu.VMEM((6 * tok, dl), BF16),
        pltpu.VMEM((6 * tok, dl), BF16),
        pltpu.VMEM((8 * 8, tok), F32),
        pltpu.VMEM((rows, wide), BF16),
        pltpu.VMEM((BR, wide), BF16),
        pltpu.VMEM((2 * rows, dl), BF16),
        pltpu.VMEM((2 * rows, dl), BF16),
        pltpu.VMEM((BR, 2 * hid), F32),
        pltpu.VMEM((halves, 2 * hid), F32),
        pltpu.VMEM((halves, 2 * hid), BF16),
        pltpu.VMEM((halves, 2 * hid), BF16),
        pltpu.VMEM((halves, 2 * hid), BF16),
        pltpu.VMEM((halves, 2 * hid), BF16),
        pltpu.VMEM((rows, 2 * hid + 128), BF16),
        pltpu.VMEM((rows, dl + 128), BF16),
        pltpu.VMEM((rows, dl + 128), BF16),
        pltpu.VMEM((14 * tok, dl // 2), BF16),
        pltpu.VMEM((14 * tok, dl // 2), BF16),
        pltpu.VMEM((8 * 8, tok), F32),
        pltpu.VMEM((8 * 8, tok), F32),
        pltpu.VMEM((2 * tok, dl // 2), F32),
        pltpu.VMEM((dl, hid), BF16),
        pltpu.VMEM((hid, dl), BF16),
        pltpu.VMEM((dl, hid), BF16),
        pltpu.VMEM((hid, dl), BF16),
        pltpu.VMEM((2 * LAST, tok), BF16),
        pltpu.VMEM((LAST, tok), BF16),
        pltpu.VMEM((2 * LAST, dl), BF16),
        pltpu.VMEM((2 * LAST, dl), BF16),
        pltpu.VMEM((BR, LAST), BF16),
    ]
    scratch += [
        pltpu.SemaphoreType.DMA((4,)),
        pltpu.SemaphoreType.DMA((4,)),
        pltpu.SemaphoreType.DMA((4,)),
    ]
    for count in (24, 2 * TILES + 2, 3 * TILES, TILES, 14, 8):
        scratch += [pltpu.SemaphoreType.DMA((count,))] * 2
    grad_tokens, scores, grad_up, grad_down = pl.pallas_call(
        kernel,
        out_shape=(
            jax.ShapeDtypeStruct((tok, dl), BF16),
            jax.ShapeDtypeStruct((2, tok), F32),
            jax.ShapeDtypeStruct((dl, hid), BF16),
            jax.ShapeDtypeStruct((hid, dl), BF16),
        ),
        in_specs=[vmem] * 4 + [hbm] * 2,
        out_specs=(vmem, vmem, hbm, hbm),
        scratch_shapes=scratch,
        compiler_params=pltpu.CompilerParams(
            collective_id=0, has_side_effects=True, vmem_limit_bytes=60 * 2**20
        ),
    )(tokens, cotangent, gate_prob.T, expert_ids.T, w_up[0], w_down[0])
    made = (grad_tokens, scores, grad_up, grad_down)
    grad_tokens, scores, grad_up, grad_down = pl.pallas_call(
        hand_over,
        out_shape=tuple(jax.ShapeDtypeStruct(a.shape, a.dtype) for a in made),
        in_specs=[hbm] * 4,
        out_specs=(hbm,) * 4,
        scratch_shapes=[pltpu.VMEM(a.shape, a.dtype) for a in made] + [pltpu.SemaphoreType.DMA((2, 4, PIECES))],
    )(*made)
    return grad_tokens, scores.T, grad_up[None], grad_down[None]


def solution(mesh):
    in_specs = (
        P("ep", "dp"),
        P("ep", "dp"),
        P("ep", None),
        P("ep", None),
        P("ep", "dp", None),
        P("ep", None, "dp"),
    )
    out_specs = (P("ep", "dp"), P("ep", None), P("ep", "dp", None), P("ep", None, "dp"))
    return jax.shard_map(
        on_device, mesh=mesh, in_specs=in_specs, out_specs=out_specs, check_vma=False
    )
```

```python
import functools

import jax
import jax.numpy as jnp
from jax import lax
from jax.experimental import pallas as pl
from jax.experimental.pallas import tpu as pltpu
from jax.sharding import PartitionSpec as P

MESH = pl.DeviceIdType.MESH
F32, BF16 = jnp.float32, jnp.bfloat16
NY, NX, NZ = 4, 2, 8
NO = NY * NX
CAP = 10
TR = 16
TILES = NZ * CAP // TR
BR = NO * TR
LAST = NO * CAP
DISP = (0, -1, 1, -2, 2, -3, 3, 4)
SPANS = tuple(
    tuple(sorted({(TR * t + i) // CAP for i in range(TR)})) for t in range(TILES)
)
FAR_TO_NEAR = ((7, 6, 4, 2), (7, 5, 3, 1))
LC = 256
PIECES = 4


def dot(a, b, ca=1, cb=0):
    return lax.dot_general(a, b, (((ca,), (cb,)), ((), ())), preferred_element_type=F32)


def kernel(
    x_ref, c_ref, gate_ref, ids_ref, up_hbm, down_hbm,
    gx_ref, gs_ref, gu_hbm, gd_hbm,
    xa, ca, ma, smat, gmat, sx, rx, puf, own, ps, pr, qs, qr, ag, dxs, dxr,
    rso, rsi, sco, sci, tf, up_ref, down_ref, gu_ref, gd_ref, lmat, lgate, lout, lin, pm, w_s,
    last_s, last_r,
    ag_s, ag_r, yx_s, yx_r, dp_s, dp_r, rt_s, rt_r, rs_s, rs_r, sc_s, sc_r,
):
    tok, dl = x_ref.shape
    hid = up_ref.shape[1]
    slots = TILES * BR
    half_rows = BR // 2
    half_lanes = dl // 2
    me = lax.axis_index("ep")
    dp = lax.axis_index("dp")
    z, yx = me % NZ, me // NZ
    y, x = yx // NX, yx % NX
    core, hi = dp % 2, dp // 2
    neighbour = (yx * NZ + (z + 1) % NZ, yx * NZ + (z + NZ - 1) % NZ)
    core_peer, hi_peer = hi * 2 + (1 - core), (1 - hi) * 2 + core

    def at_offset(o, sign):
        dy, dx = o // NX, o % NX
        there = ((y + sign * dy + NY) % NY) * NX + (x + sign * dx + NX) % NX
        return there * NZ + z

    def remote(src, dst, ss, rs, device):
        return pltpu.make_async_remote_copy(
            src_ref=src, dst_ref=dst, send_sem=ss, recv_sem=rs, device_id=device, device_id_type=MESH
        )

    barrier = pltpu.get_barrier_semaphore()
    peers = [{"ep": n} for n in neighbour]
    peers += [{"ep": at_offset(o, 1)} for o in range(1, NO)]
    peers += [{"dp": core_peer}, {"dp": hi_peer}]
    for peer in peers:
        pl.semaphore_signal(barrier, inc=1, device_id=peer, device_id_type=MESH)

    loads = [
        pltpu.make_async_copy(up_hbm, up_ref, w_s.at[0]),
        pltpu.make_async_copy(down_hbm, down_ref, w_s.at[1]),
    ]
    for load in loads:
        load.start()

    gate_rows = gate_ref[...].astype(F32)
    ids_rows = ids_ref[...].astype(F32)
    ids = [ids_rows[k : k + 1, :] for k in range(2)]
    expert_no = lax.broadcasted_iota(jnp.int32, (NO * NZ // 2, tok), 0).astype(F32)
    hot = [jnp.where(expert_no == ids[k], 1.0, 0.0) for k in range(2)]
    earlier = lax.broadcasted_iota(jnp.int32, (tok, tok), 0) < lax.broadcasted_iota(
        jnp.int32, (tok, tok), 1
    )
    before = dot((hot[0] + hot[1]).astype(BF16), jnp.where(earlier, 1.0, 0.0).astype(BF16))
    code = [
        ids[k] * 16.0 + jnp.sum(before * hot[k], axis=0, keepdims=True) for k in range(2)
    ]
    line = lax.broadcasted_iota(jnp.int32, (8, tok), 0)
    upper = jnp.where(line == 0, code[0], code[1])
    ma[0:8, :] = jnp.where(line < 2, upper, jnp.where(line == 2, gate_rows[0:1, :], gate_rows[1:2, :]))
    pl.semaphore_wait(barrier, len(peers))

    def block(ref, own_ref, j):
        return own_ref if j == 0 else ref.at[(j - 1) * tok : j * tok, :]

    def gather_sent(way, step, n):
        return step < 3 or (way == 0 and n == 2)

    def gather_copy(way, step, n):
        src = 0 if step == 0 else 2 * step - 1 + way
        dst = 7 if step == 3 else 2 * step + 1 + way
        if n == 2:
            a, b = ma.at[src * 8 : src * 8 + 8, :], ma.at[dst * 8 : dst * 8 + 8, :]
        else:
            ref, own_ref = ((xa, x_ref), (ca, c_ref))[n]
            a, b = block(ref, own_ref, src), block(ref, own_ref, dst)
        sem = (way * 4 + step) * 3 + n
        return remote(a, b, ag_s.at[sem], ag_r.at[sem], {"ep": neighbour[way]})

    def gather_start():
        for n in (2, 0, 1):
            for way in range(2):
                gather_copy(way, 0, n).start()

    def gather_next(step, part):
        for n in ((2, 0), (1,))[part]:
            for way in (part, 1 - part):
                if gather_sent(way, step, n):
                    gather_copy(way, step, n).wait_recv()
                if step < 3 and gather_sent(way, step + 1, n):
                    gather_copy(way, step + 1, n).start()
                if step == 2 and n == way:
                    last_hop(way)

    def last_copy(way, h):
        n = way * 2 + h
        rows, lanes = pl.ds(way * LAST, LAST), pl.ds(h * half_lanes, half_lanes)
        return remote(
            lout.at[rows, lanes], lin.at[rows, lanes], last_s.at[n], last_r.at[n], {"ep": neighbour[way]}
        )

    def last_hop(way):
        j = 5 + way
        spot = lax.broadcasted_iota(jnp.int32, (LAST, tok), 0)
        o_at = (spot * 205) >> 11
        there = ((y + (o_at >> 1)) & (NY - 1)) * NX + ((x + (o_at & 1)) & (NX - 1))
        pair = ((z + (1, NZ - 1)[way]) % NZ) // 2
        want = ((there * (NZ // 2) + pair) * 16 + (spot - o_at * CAP)).astype(F32)
        first, second = [want == ma[j * 8 + k : j * 8 + k + 1, :] for k in range(2)]
        mine = slice(way * LAST, (way + 1) * LAST)
        lmat[mine, :] = jnp.where(jnp.logical_or(first, second), 1.0, 0.0).astype(BF16)
        if way == 1:
            gates = [ma[j * 8 + 2 + k : j * 8 + 3 + k, :] for k in range(2)]
            lgate[...] = jnp.where(first, gates[0], jnp.where(second, gates[1], 0.0)).astype(BF16)
        ref, own_ref = ((xa, x_ref), (ca, c_ref))[way]

        def piece(i, carry):
            lanes = pl.ds(pl.multiple_of(i * 128, 128), 128)
            pick = lmat[mine, :] if way == 0 else lgate[...]
            lout[mine, lanes] = dot(pick, block(ref, own_ref, j)[:, lanes]).astype(BF16)
            return carry

        each = half_lanes // 128
        for h in range(2):
            lax.fori_loop(h * each, (h + 1) * each, piece, 0)
            last_copy(way, h).start()

    rho = lax.broadcasted_iota(jnp.int32, (BR, tok), 0)
    o_of = rho >> 4
    i_of = rho & 15
    to_yx = ((y + (o_of >> 1)) & (NY - 1)) * NX + ((x + (o_of & 1)) & (NX - 1))
    expert_of = to_yx * (NZ // 2) + z // 2

    def matches(t, j):
        rank = i_of + (TR * t - CAP * j)
        good = jnp.logical_and(rank >= 0, rank < CAP)
        want = jnp.where(good, expert_of * 16 + rank, -1).astype(F32)
        return [want == ma[j * 8 + k : j * 8 + k + 1, :] for k in range(2)]

    def rows_of(t):
        return pl.ds(t * BR, BR)

    def yx_copy(t, part, h, first, count, o):
        rows = pl.ds(part * slots + t * BR + first, count)
        lanes = pl.ds(0, dl)
        n = 2 * t + part
        if t == TILES - 1:
            lanes = pl.ds(h * half_lanes, half_lanes)
            n += part + h
        return remote(
            sx.at[rows, lanes], rx.at[rows, lanes], yx_s.at[n], yx_r.at[n], {"ep": at_offset(o, 1)}
        )

    def yx_all(t, part):
        return [yx_copy(t, part, h, TR, BR - TR, 1) for h in range(2 if t == TILES - 1 else 1)]

    def pick_matrices(t, part):
        for n, j in enumerate(SPANS[t]):
            first, second = matches(t, j)
            lanes = pl.ds(n * tok, tok)
            if part == 0:
                smat[rows_of(t), lanes] = jnp.where(jnp.logical_or(first, second), 1.0, 0.0).astype(BF16)
            elif j < 7:
                gates = [ma[j * 8 + 2 + k : j * 8 + 3 + k, :] for k in range(2)]
                gmat[:, lanes] = jnp.where(first, gates[0], jnp.where(second, gates[1], 0.0)).astype(BF16)

    def select(t, part, h=0):
        if h == 0:
            pick_matrices(t, part)
        base = part * slots + t * BR
        last = t == TILES - 1
        width = 128 if last else LC

        def piece(i, carry):
            lanes = pl.ds(pl.multiple_of(i * width, width), width)
            total = None
            for n, j in enumerate(SPANS[t]):
                if j == 7:
                    one = dot(pm[...], lin[part * LAST : (part + 1) * LAST, lanes])
                elif part == 0:
                    one = dot(smat[rows_of(t), n * tok : (n + 1) * tok], block(xa, x_ref, j)[:, lanes])
                else:
                    one = dot(gmat[:, n * tok : (n + 1) * tok], block(ca, c_ref, j)[:, lanes])
                total = one if total is None else total + one
            sx[pl.ds(base, BR), lanes] = total.astype(BF16)
            return carry

        each = half_lanes // 128
        lax.fori_loop(*((h * each, (h + 1) * each) if last else (0, dl // LC)), piece, 0)
        for o in range(1, NO):
            yx_copy(t, part, h, o * TR, TR, o).start()
        span = slice(h * half_lanes, (h + 1) * half_lanes) if last else slice(0, dl)
        rx[base : base + TR, span] = sx[base : base + TR, span]

    def dp_copy(t, stage):
        sems = (dp_s.at[t * 3 + stage], dp_r.at[t * 3 + stage])
        here = pl.ds(t * half_rows, half_rows)
        if stage == 0:
            return remote(ps.at[here, :], pr.at[here, :], *sems, {"dp": core_peer})
        if stage == 1:
            return remote(qs.at[here, :], qr.at[here, :], *sems, {"dp": hi_peer})
        mine = pl.ds(pl.multiple_of(t * BR + core * half_rows, half_rows), half_rows)
        return remote(ag.at[mine, :], ag.at[mine, :], *sems, {"dp": core_peer})

    def hidden(t):
        for half in range(2):
            for copy in yx_all(t, half):
                copy.wait_recv()

        def part(i, carry):
            cols = pl.ds(pl.multiple_of(i * LC, LC), LC)
            later = pl.ds(pl.multiple_of(hid + i * LC, LC), LC)
            puf[:, cols] = dot(rx[rows_of(t), :], up_ref[:, cols])
            puf[:, later] = dot(rx[pl.ds(slots + t * BR, BR), :], down_ref[cols, :], 1, 1)
            return carry

        lax.fori_loop(0, hid // LC, part, 0)
        here = pl.ds(t * half_rows, half_rows)
        theirs = pl.ds(pl.multiple_of((1 - core) * half_rows, half_rows), half_rows)
        mine = pl.ds(pl.multiple_of(core * half_rows, half_rows), half_rows)
        ps[here, :] = puf[theirs, :].astype(BF16)
        dp_copy(t, 0).start()
        own[here, :] = puf[mine, :]

    def chip_sum(t):
        dp_copy(t, 0).wait_recv()
        here = pl.ds(t * half_rows, half_rows)
        qs[here, :] = (own[here, :] + pr[here, :].astype(F32)).astype(BF16)
        dp_copy(t, 1).start()

    def activate(t):
        dp_copy(t, 1).wait_recv()
        here = pl.ds(t * half_rows, half_rows)
        mine = pl.ds(pl.multiple_of(t * BR + core * half_rows, half_rows), half_rows)
        preact = qs[here, 0:hid].astype(F32) + qr[here, 0:hid].astype(F32)
        upstream = qs[here, hid : 2 * hid].astype(F32) + qr[here, hid : 2 * hid].astype(F32)
        sig = 1.0 / (1.0 + jnp.exp(-preact))
        act = (preact * sig).astype(BF16)
        ag[mine, 0:hid] = act
        ag[mine, hid : 2 * hid] = (upstream * (sig * (1.0 + preact * (1.0 - sig)))).astype(BF16)
        score = jnp.sum(act.astype(F32) * upstream, axis=1, keepdims=True)
        ag[mine, 2 * hid : 2 * hid + 128] = jnp.broadcast_to(score, (half_rows, 128)).astype(BF16)
        dp_copy(t, 2).start()

    def back_copy(t, o):
        rows = pl.ds(t * BR + o * TR, TR)
        return remote(dxs.at[rows, :], dxr.at[rows, :], rt_s.at[t], rt_r.at[t], {"ep": at_offset(o, -1)})

    def back_all(t):
        rows = pl.ds(t * BR + TR, BR - TR)
        return remote(dxs.at[rows, :], dxr.at[rows, :], rt_s.at[t], rt_r.at[t], {"ep": at_offset(1, -1)})

    def back_rows(t):
        dp_copy(t, 2).wait_recv()

        def part(i, carry):
            cols = pl.ds(pl.multiple_of(i * LC, LC), LC)
            dxs[rows_of(t), cols] = dot(ag[rows_of(t), hid : 2 * hid], up_ref[cols, :], 1, 1).astype(BF16)
            return carry

        lax.fori_loop(0, dl // LC, part, 0)
        dxs[rows_of(t), dl : dl + 128] = ag[rows_of(t), 2 * hid : 2 * hid + 128]

    def send_back(t):
        for o in range(1, NO):
            back_copy(t, o).start()
        dxr[t * BR : t * BR + TR, :] = dxs[t * BR : t * BR + TR, :]

    def token_sum(j, lo, hi_lane):
        total = None
        for t in range(TILES):
            if j in SPANS[t]:
                n = SPANS[t].index(j)
                one = dot(smat[rows_of(t), n * tok : (n + 1) * tok], dxr[rows_of(t), lo:hi_lane], 0, 0)
                total = one if total is None else total + one
        return total

    def score_sum(j):
        sums = [0.0, 0.0]
        for t in range(TILES):
            if j in SPANS[t]:
                value = dxr[rows_of(t), dl : dl + 128].astype(F32)
                for k, hit in enumerate(matches(t, j)):
                    sums[k] = sums[k] + jnp.sum(jnp.where(hit, value, 0.0), axis=0, keepdims=True)
        return jnp.where(line == 0, sums[0], jnp.where(line == 1, sums[1], 0.0))

    def lanes_of(way, m):
        return half_lanes if (way + m) % 2 else 0

    def sum_rows(way, m):
        return slice((way * 7 + m) * tok, (way * 7 + m + 1) * tok)

    def sum_copy(way, m):
        n = way * 7 + m
        rows = pl.ds(n * tok, tok if m else LAST)
        return remote(rso.at[rows, :], rsi.at[rows, :], rs_s.at[n], rs_r.at[n], {"ep": neighbour[way]})

    def score_copy(way, step):
        n = way * 4 + step
        rows = pl.ds(n * 8, 8)
        return remote(sco.at[rows, :], sci.at[rows, :], sc_s.at[n], sc_r.at[n], {"ep": neighbour[way]})

    def scored(way, step):
        return step > 0 or way == 0

    def sum_ready(way, m):
        lo = lanes_of(way, m)
        if m == 0:
            tf[way * tok : way * tok + LAST, :] = dot(
                pm[...], dxr[rows_of(TILES - 1), lo : lo + half_lanes], 0, 0
            )
            return
        tf[way * tok : (way + 1) * tok, :] = token_sum(FAR_TO_NEAR[way][(m + 1) // 2], lo, lo + half_lanes)

    def sum_next(way, m):
        count = tok if m else LAST
        total = tf[way * tok : way * tok + count, :]
        first = (way * 7 + m) * tok
        if m >= 2:
            sum_copy(way, m - 2).wait_recv()
        if m == 2:
            came = rsi[first - 2 * tok : first - 2 * tok + LAST, :]
            total = total + dot(lmat[(1 - way) * LAST : (2 - way) * LAST, :], came, 0, 0)
        elif m > 2:
            total = total + rsi[sum_rows(way, m - 2), :].astype(F32)
        rso[first : first + count, :] = total.astype(BF16)
        sum_copy(way, m).start()

    def score_next(way, step):
        n = way * 4 + step
        here = score_sum(FAR_TO_NEAR[way][step])
        if step > 0 and scored(way, step - 1):
            score_copy(way, step - 1).wait_recv()
            here = here + sci[n * 8 - 8 : n * 8, :]
        sco[n * 8 : n * 8 + 8, :] = here
        score_copy(way, step).start()

    def up_gradient():
        def part(i, carry):
            cols = pl.ds(pl.multiple_of(i * LC, LC), LC)
            gu_ref[cols, :] = dot(rx[0:slots, cols], ag[:, hid : 2 * hid], 0, 0).astype(BF16)
            return carry

        lax.fori_loop(0, dl // LC, part, 0)

    def down_gradient():
        def part(i, carry):
            cols = pl.ds(pl.multiple_of(i * LC, LC), LC)
            gd_ref[:, cols] = dot(ag[:, 0:hid], rx[slots : 2 * slots, cols], 0, 0).astype(BF16)
            return carry

        lax.fori_loop(0, dl // LC, part, 0)

    gather_start()
    gather_next(0, 0)
    select(0, 0)
    gather_next(0, 1)
    select(0, 1)
    gather_next(1, 0)
    select(1, 0)
    select(2, 0)
    slot_row = lax.broadcasted_iota(jnp.int32, (BR, LAST), 0)
    rank_row = (slot_row & 15) - (TR - CAP)
    spot_of = jnp.where(rank_row >= 0, (slot_row >> 4) * CAP + rank_row, -1)
    pm[...] = jnp.where(spot_of == lax.broadcasted_iota(jnp.int32, (BR, LAST), 1), 1.0, 0.0).astype(BF16)
    for load in loads:
        load.wait()
    hidden(0)
    chip_sum(0)
    gather_next(1, 1)
    select(1, 1)
    select(2, 1)
    activate(0)
    back_rows(0)
    gather_next(2, 0)
    select(3, 0)
    hidden(1)
    chip_sum(1)
    gather_next(2, 1)
    select(3, 1)
    activate(1)
    hidden(2)
    chip_sum(2)
    gather_copy(0, 3, 2).wait_recv()
    for h in range(2):
        for part in range(2):
            last_copy(part, h).wait_recv()
            select(4, part, h)
    hidden(3)
    chip_sum(3)
    hidden(4)
    chip_sum(4)
    activate(2)
    activate(3)
    back_rows(3)
    activate(4)
    send_back(3)
    back_rows(4)
    send_back(4)
    back_rows(2)
    send_back(2)
    back_rows(1)
    send_back(1)
    send_back(0)
    stores = [
        pltpu.make_async_copy(gu_ref, gu_hbm, w_s.at[2]),
        pltpu.make_async_copy(gd_ref, gd_hbm, w_s.at[3]),
    ]
    up_gradient()
    stores[0].start()
    back_all(4).wait_recv()
    for way in range(2):
        sum_ready(way, 0)
        sum_next(way, 0)
    back_all(3).wait_recv()
    for m in range(1, 7):
        if m == 3:
            back_all(2).wait_recv()
        for way in range(2):
            if (way, m) == (1, 3):
                back_all(1).wait_recv()
            if (way, m) == (1, 5):
                back_all(0).wait_recv()
            sum_ready(way, m)
            sum_next(way, m)
        if m == 1:
            down_gradient()
            stores[1].start()
        if m % 2 == 0:
            for way in range(2):
                if m == 2 and way == 0:
                    score_next(0, 0)
                score_next(way, m // 2)
    for n, lo in enumerate((0, half_lanes)):
        tf[n * tok : (n + 1) * tok, :] = token_sum(0, lo, lo + half_lanes)
    scores = score_sum(0)
    for m in (5, 6):
        for way in range(2):
            sum_copy(way, m).wait_recv()
    for m in (5, 6):
        lo = lanes_of(0, m)
        n = lo // half_lanes
        gx_ref[:, lo : lo + half_lanes] = (
            tf[n * tok : (n + 1) * tok, :]
            + rsi[sum_rows(0, m), :].astype(F32)
            + rsi[sum_rows(1, 11 - m), :].astype(F32)
        ).astype(BF16)
    for way in range(2):
        score_copy(way, 3).wait_recv()
    gates = jnp.where(line == 0, ma[2:3, :], jnp.where(line == 1, ma[3:4, :], 1.0))
    gs_ref[...] = ((scores + sci[24:32, :] + sci[56:64, :]) / gates)[0:2, :]

    for way in range(2):
        for step in range(4):
            for n in range(3):
                if gather_sent(way, step, n):
                    gather_copy(way, step, n).wait_send()
            if scored(way, step):
                score_copy(way, step).wait_send()
        for m in range(7):
            sum_copy(way, m).wait_send()
        for h in range(2):
            last_copy(way, h).wait_send()
    for t in range(TILES):
        for part in range(2):
            for copy in yx_all(t, part):
                copy.wait_send()
        back_all(t).wait_send()
        for stage in range(3):
            dp_copy(t, stage).wait_send()
    for store in stores:
        store.wait()


def hand_over(*refs):
    sems = refs[12]
    loads, stores = [], []
    for n in range(4):
        pieces = PIECES if refs[n].shape[0] % (16 * PIECES) == 0 else 1
        size = refs[n].shape[0] // pieces
        for i in range(pieces):
            rows = pl.ds(i * size, size)
            held = refs[8 + n].at[rows, :]
            loads.append(pltpu.make_async_copy(refs[n].at[rows, :], held, sems.at[0, n, i]))
            stores.append(pltpu.make_async_copy(held, refs[4 + n].at[rows, :], sems.at[1, n, i]))
    for load in loads:
        load.start()
    for load, store in zip(loads, stores):
        load.wait()
        store.start()
    for store in stores:
        store.wait()


def on_device(tokens, cotangent, gate_prob, expert_ids, w_up, w_down):
    tok, dl = tokens.shape
    hid = w_up.shape[2]
    vmem = pl.BlockSpec(memory_space=pltpu.VMEM)
    hbm = pl.BlockSpec(memory_space=pl.ANY)
    rows = TILES * BR
    halves = rows // 2
    wide = max(len(s) for s in SPANS) * tok
    scratch = [
        pltpu.VMEM((6 * tok, dl), BF16),
        pltpu.VMEM((6 * tok, dl), BF16),
        pltpu.VMEM((8 * 8, tok), F32),
        pltpu.VMEM((rows, wide), BF16),
        pltpu.VMEM((BR, wide), BF16),
        pltpu.VMEM((2 * rows, dl), BF16),
        pltpu.VMEM((2 * rows, dl), BF16),
        pltpu.VMEM((BR, 2 * hid), F32),
        pltpu.VMEM((halves, 2 * hid), F32),
        pltpu.VMEM((halves, 2 * hid), BF16),
        pltpu.VMEM((halves, 2 * hid), BF16),
        pltpu.VMEM((halves, 2 * hid), BF16),
        pltpu.VMEM((halves, 2 * hid), BF16),
        pltpu.VMEM((rows, 2 * hid + 128), BF16),
        pltpu.VMEM((rows, dl + 128), BF16),
        pltpu.VMEM((rows, dl + 128), BF16),
        pltpu.VMEM((14 * tok, dl // 2), BF16),
        pltpu.VMEM((14 * tok, dl // 2), BF16),
        pltpu.VMEM((8 * 8, tok), F32),
        pltpu.VMEM((8 * 8, tok), F32),
        pltpu.VMEM((2 * tok, dl // 2), F32),
        pltpu.VMEM((dl, hid), BF16),
        pltpu.VMEM((hid, dl), BF16),
        pltpu.VMEM((dl, hid), BF16),
        pltpu.VMEM((hid, dl), BF16),
        pltpu.VMEM((2 * LAST, tok), BF16),
        pltpu.VMEM((LAST, tok), BF16),
        pltpu.VMEM((2 * LAST, dl), BF16),
        pltpu.VMEM((2 * LAST, dl), BF16),
        pltpu.VMEM((BR, LAST), BF16),
    ]
    scratch += [
        pltpu.SemaphoreType.DMA((4,)),
        pltpu.SemaphoreType.DMA((4,)),
        pltpu.SemaphoreType.DMA((4,)),
    ]
    for count in (24, 2 * TILES + 2, 3 * TILES, TILES, 14, 8):
        scratch += [pltpu.SemaphoreType.DMA((count,))] * 2
    grad_tokens, scores, grad_up, grad_down = pl.pallas_call(
        kernel,
        out_shape=(
            jax.ShapeDtypeStruct((tok, dl), BF16),
            jax.ShapeDtypeStruct((2, tok), F32),
            jax.ShapeDtypeStruct((dl, hid), BF16),
            jax.ShapeDtypeStruct((hid, dl), BF16),
        ),
        in_specs=[vmem] * 4 + [hbm] * 2,
        out_specs=(vmem, vmem, hbm, hbm),
        scratch_shapes=scratch,
        compiler_params=pltpu.CompilerParams(
            collective_id=0, has_side_effects=True, vmem_limit_bytes=60 * 2**20
        ),
    )(tokens, cotangent, gate_prob.T, expert_ids.T, w_up[0], w_down[0])
    made = (grad_tokens, scores, grad_up, grad_down)
    grad_tokens, scores, grad_up, grad_down = pl.pallas_call(
        hand_over,
        out_shape=tuple(jax.ShapeDtypeStruct(a.shape, a.dtype) for a in made),
        in_specs=[hbm] * 4,
        out_specs=(hbm,) * 4,
        scratch_shapes=[pltpu.VMEM(a.shape, a.dtype) for a in made] + [pltpu.SemaphoreType.DMA((2, 4, PIECES))],
    )(*made)
    return grad_tokens, scores.T, grad_up[None], grad_down[None]


def solution(mesh):
    in_specs = (
        P("ep", "dp"),
        P("ep", "dp"),
        P("ep", None),
        P("ep", None),
        P("ep", "dp", None),
        P("ep", None, "dp"),
    )
    out_specs = (P("ep", "dp"), P("ep", None), P("ep", "dp", None), P("ep", None, "dp"))
    return jax.shard_map(
        on_device, mesh=mesh, in_specs=in_specs, out_specs=out_specs, check_vma=False
    )
```

```python
import functools

import jax
import jax.numpy as jnp
from jax import lax
from jax.experimental import pallas as pl
from jax.experimental.pallas import tpu as pltpu
from jax.sharding import PartitionSpec as P

MESH = pl.DeviceIdType.MESH
F32, BF16 = jnp.float32, jnp.bfloat16
NY, NX, NZ = 4, 2, 8
NO = NY * NX
CAP = 10
TR = 16
TILES = NZ * CAP // TR
BR = NO * TR
LAST = NO * CAP
DISP = (0, -1, 1, -2, 2, -3, 3, 4)
SPANS = tuple(
    tuple(sorted({(TR * t + i) // CAP for i in range(TR)})) for t in range(TILES)
)
FAR_TO_NEAR = ((7, 6, 4, 2), (7, 5, 3, 1))
LC = 256
PIECES = 4


def dot(a, b, ca=1, cb=0):
    return lax.dot_general(a, b, (((ca,), (cb,)), ((), ())), preferred_element_type=F32)


def kernel(
    x_ref, c_ref, gate_ref, ids_ref, up_hbm, down_hbm,
    gx_ref, gs_ref, gu_hbm, gd_hbm,
    xa, ca, ma, smat, gmat, sx, rx, puf, own, ps, pr, qs, qr, ag, dxs, dxr,
    rso, rsi, sco, sci, tf, up_ref, down_ref, gu_ref, gd_ref, lmat, lgate, lout, lin, pm, w_s,
    last_s, last_r,
    ag_s, ag_r, yx_s, yx_r, dp_s, dp_r, rt_s, rt_r, rs_s, rs_r, sc_s, sc_r,
):
    tok, dl = x_ref.shape
    hid = up_ref.shape[1]
    slots = TILES * BR
    half_rows = BR // 2
    half_lanes = dl // 2
    me = lax.axis_index("ep")
    dp = lax.axis_index("dp")
    z, yx = me % NZ, me // NZ
    y, x = yx // NX, yx % NX
    core, hi = dp % 2, dp // 2
    neighbour = (yx * NZ + (z + 1) % NZ, yx * NZ + (z + NZ - 1) % NZ)
    core_peer, hi_peer = hi * 2 + (1 - core), (1 - hi) * 2 + core

    def at_offset(o, sign):
        dy, dx = o // NX, o % NX
        there = ((y + sign * dy + NY) % NY) * NX + (x + sign * dx + NX) % NX
        return there * NZ + z

    def remote(src, dst, ss, rs, device):
        return pltpu.make_async_remote_copy(
            src_ref=src, dst_ref=dst, send_sem=ss, recv_sem=rs, device_id=device, device_id_type=MESH
        )

    barrier = pltpu.get_barrier_semaphore()
    peers = [{"ep": n} for n in neighbour]
    peers += [{"ep": at_offset(o, 1)} for o in range(1, NO)]
    peers += [{"dp": core_peer}, {"dp": hi_peer}]
    for peer in peers:
        pl.semaphore_signal(barrier, inc=1, device_id=peer, device_id_type=MESH)

    loads = [
        pltpu.make_async_copy(up_hbm, up_ref, w_s.at[0]),
        pltpu.make_async_copy(down_hbm, down_ref, w_s.at[1]),
    ]
    for load in loads:
        load.start()

    gate_rows = gate_ref[...].astype(F32)
    ids_rows = ids_ref[...].astype(F32)
    ids = [ids_rows[k : k + 1, :] for k in range(2)]
    expert_no = lax.broadcasted_iota(jnp.int32, (NO * NZ // 2, tok), 0).astype(F32)
    hot = [jnp.where(expert_no == ids[k], 1.0, 0.0) for k in range(2)]
    earlier = lax.broadcasted_iota(jnp.int32, (tok, tok), 0) < lax.broadcasted_iota(
        jnp.int32, (tok, tok), 1
    )
    before = dot((hot[0] + hot[1]).astype(BF16), jnp.where(earlier, 1.0, 0.0).astype(BF16))
    code = [
        ids[k] * 16.0 + jnp.sum(before * hot[k], axis=0, keepdims=True) for k in range(2)
    ]
    line = lax.broadcasted_iota(jnp.int32, (8, tok), 0)
    upper = jnp.where(line == 0, code[0], code[1])
    ma[0:8, :] = jnp.where(line < 2, upper, jnp.where(line == 2, gate_rows[0:1, :], gate_rows[1:2, :]))
    pl.semaphore_wait(barrier, len(peers))

    def block(ref, own_ref, j):
        return own_ref if j == 0 else ref.at[(j - 1) * tok : j * tok, :]

    def gather_sent(way, step, n):
        return step < 3 or (way == 0 and n == 2)

    def gather_copy(way, step, n):
        src = 0 if step == 0 else 2 * step - 1 + way
        dst = 7 if step == 3 else 2 * step + 1 + way
        if n == 2:
            a, b = ma.at[src * 8 : src * 8 + 8, :], ma.at[dst * 8 : dst * 8 + 8, :]
        else:
            ref, own_ref = ((xa, x_ref), (ca, c_ref))[n]
            a, b = block(ref, own_ref, src), block(ref, own_ref, dst)
        sem = (way * 4 + step) * 3 + n
        return remote(a, b, ag_s.at[sem], ag_r.at[sem], {"ep": neighbour[way]})

    def gather_start():
        for n in (2, 0, 1):
            for way in range(2):
                gather_copy(way, 0, n).start()

    def gather_next(step, part):
        for n in ((2, 0), (1,))[part]:
            for way in (part, 1 - part):
                if gather_sent(way, step, n):
                    gather_copy(way, step, n).wait_recv()
                if step < 3 and gather_sent(way, step + 1, n):
                    gather_copy(way, step + 1, n).start()
                if step == 2 and n == way:
                    last_hop(way)

    def last_copy(way, h):
        n = way * 2 + h
        rows, lanes = pl.ds(way * LAST, LAST), pl.ds(h * half_lanes, half_lanes)
        return remote(
            lout.at[rows, lanes], lin.at[rows, lanes], last_s.at[n], last_r.at[n], {"ep": neighbour[way]}
        )

    def last_hop(way):
        j = 5 + way
        spot = lax.broadcasted_iota(jnp.int32, (LAST, tok), 0)
        o_at = (spot * 205) >> 11
        there = ((y + (o_at >> 1)) & (NY - 1)) * NX + ((x + (o_at & 1)) & (NX - 1))
        pair = ((z + (1, NZ - 1)[way]) % NZ) // 2
        want = ((there * (NZ // 2) + pair) * 16 + (spot - o_at * CAP)).astype(F32)
        first, second = [want == ma[j * 8 + k : j * 8 + k + 1, :] for k in range(2)]
        mine = slice(way * LAST, (way + 1) * LAST)
        lmat[mine, :] = jnp.where(jnp.logical_or(first, second), 1.0, 0.0).astype(BF16)
        if way == 1:
            gates = [ma[j * 8 + 2 + k : j * 8 + 3 + k, :] for k in range(2)]
            lgate[...] = jnp.where(first, gates[0], jnp.where(second, gates[1], 0.0)).astype(BF16)
        ref, own_ref = ((xa, x_ref), (ca, c_ref))[way]

        def piece(i, carry):
            lanes = pl.ds(pl.multiple_of(i * 128, 128), 128)
            pick = lmat[mine, :] if way == 0 else lgate[...]
            lout[mine, lanes] = dot(pick, block(ref, own_ref, j)[:, lanes]).astype(BF16)
            return carry

        each = half_lanes // 128
        for h in range(2):
            lax.fori_loop(h * each, (h + 1) * each, piece, 0)
            last_copy(way, h).start()

    rho = lax.broadcasted_iota(jnp.int32, (BR, tok), 0)
    o_of = rho >> 4
    i_of = rho & 15
    to_yx = ((y + (o_of >> 1)) & (NY - 1)) * NX + ((x + (o_of & 1)) & (NX - 1))
    expert_of = to_yx * (NZ // 2) + z // 2

    def matches(t, j):
        rank = i_of + (TR * t - CAP * j)
        good = jnp.logical_and(rank >= 0, rank < CAP)
        want = jnp.where(good, expert_of * 16 + rank, -1).astype(F32)
        return [want == ma[j * 8 + k : j * 8 + k + 1, :] for k in range(2)]

    def rows_of(t):
        return pl.ds(t * BR, BR)

    def yx_copy(t, part, h, first, count, o):
        rows = pl.ds(part * slots + t * BR + first, count)
        lanes = pl.ds(0, dl)
        n = 2 * t + part
        if t == TILES - 1:
            lanes = pl.ds(h * half_lanes, half_lanes)
            n += part + h
        return remote(
            sx.at[rows, lanes], rx.at[rows, lanes], yx_s.at[n], yx_r.at[n], {"ep": at_offset(o, 1)}
        )

    def yx_all(t, part):
        return [yx_copy(t, part, h, TR, BR - TR, 1) for h in range(2 if t == TILES - 1 else 1)]

    def pick_matrices(t, part):
        for n, j in enumerate(SPANS[t]):
            first, second = matches(t, j)
            lanes = pl.ds(n * tok, tok)
            if part == 0:
                smat[rows_of(t), lanes] = jnp.where(jnp.logical_or(first, second), 1.0, 0.0).astype(BF16)
            elif j < 7:
                gates = [ma[j * 8 + 2 + k : j * 8 + 3 + k, :] for k in range(2)]
                gmat[:, lanes] = jnp.where(first, gates[0], jnp.where(second, gates[1], 0.0)).astype(BF16)

    def select(t, part, h=0):
        if h == 0:
            pick_matrices(t, part)
        base = part * slots + t * BR
        last = t == TILES - 1
        width = 128 if last else LC

        def piece(i, carry):
            lanes = pl.ds(pl.multiple_of(i * width, width), width)
            total = None
            for n, j in enumerate(SPANS[t]):
                if j == 7:
                    one = dot(pm[...], lin[part * LAST : (part + 1) * LAST, lanes])
                elif part == 0:
                    one = dot(smat[rows_of(t), n * tok : (n + 1) * tok], block(xa, x_ref, j)[:, lanes])
                else:
                    one = dot(gmat[:, n * tok : (n + 1) * tok], block(ca, c_ref, j)[:, lanes])
                total = one if total is None else total + one
            sx[pl.ds(base, BR), lanes] = total.astype(BF16)
            return carry

        each = half_lanes // 128
        lax.fori_loop(*((h * each, (h + 1) * each) if last else (0, dl // LC)), piece, 0)
        for o in range(1, NO):
            yx_copy(t, part, h, o * TR, TR, o).start()
        span = slice(h * half_lanes, (h + 1) * half_lanes) if last else slice(0, dl)
        rx[base : base + TR, span] = sx[base : base + TR, span]

    def dp_copy(t, stage):
        sems = (dp_s.at[t * 3 + stage], dp_r.at[t * 3 + stage])
        here = pl.ds(t * half_rows, half_rows)
        if stage == 0:
            return remote(ps.at[here, :], pr.at[here, :], *sems, {"dp": core_peer})
        if stage == 1:
            return remote(qs.at[here, :], qr.at[here, :], *sems, {"dp": hi_peer})
        mine = pl.ds(pl.multiple_of(t * BR + core * half_rows, half_rows), half_rows)
        return remote(ag.at[mine, :], ag.at[mine, :], *sems, {"dp": core_peer})

    def hidden(t):
        for half in range(2):
            for copy in yx_all(t, half):
                copy.wait_recv()

        def part(i, carry):
            cols = pl.ds(pl.multiple_of(i * LC, LC), LC)
            later = pl.ds(pl.multiple_of(hid + i * LC, LC), LC)
            puf[:, cols] = dot(rx[rows_of(t), :], up_ref[:, cols])
            puf[:, later] = dot(rx[pl.ds(slots + t * BR, BR), :], down_ref[cols, :], 1, 1)
            return carry

        lax.fori_loop(0, hid // LC, part, 0)
        here = pl.ds(t * half_rows, half_rows)
        theirs = pl.ds(pl.multiple_of((1 - core) * half_rows, half_rows), half_rows)
        mine = pl.ds(pl.multiple_of(core * half_rows, half_rows), half_rows)
        ps[here, :] = puf[theirs, :].astype(BF16)
        dp_copy(t, 0).start()
        own[here, :] = puf[mine, :]

    def chip_sum(t):
        dp_copy(t, 0).wait_recv()
        here = pl.ds(t * half_rows, half_rows)
        qs[here, :] = (own[here, :] + pr[here, :].astype(F32)).astype(BF16)
        dp_copy(t, 1).start()

    def activate(t):
        dp_copy(t, 1).wait_recv()
        here = pl.ds(t * half_rows, half_rows)
        mine = pl.ds(pl.multiple_of(t * BR + core * half_rows, half_rows), half_rows)
        preact = qs[here, 0:hid].astype(F32) + qr[here, 0:hid].astype(F32)
        upstream = qs[here, hid : 2 * hid].astype(F32) + qr[here, hid : 2 * hid].astype(F32)
        sig = 1.0 / (1.0 + jnp.exp(-preact))
        act = (preact * sig).astype(BF16)
        ag[mine, 0:hid] = act
        ag[mine, hid : 2 * hid] = (upstream * (sig * (1.0 + preact * (1.0 - sig)))).astype(BF16)
        score = jnp.sum(act.astype(F32) * upstream, axis=1, keepdims=True)
        ag[mine, 2 * hid : 2 * hid + 128] = jnp.broadcast_to(score, (half_rows, 128)).astype(BF16)
        dp_copy(t, 2).start()

    def back_copy(t, o):
        rows = pl.ds(t * BR + o * TR, TR)
        return remote(dxs.at[rows, :], dxr.at[rows, :], rt_s.at[t], rt_r.at[t], {"ep": at_offset(o, -1)})

    def back_all(t):
        rows = pl.ds(t * BR + TR, BR - TR)
        return remote(dxs.at[rows, :], dxr.at[rows, :], rt_s.at[t], rt_r.at[t], {"ep": at_offset(1, -1)})

    def back_rows(t):
        dp_copy(t, 2).wait_recv()

        def part(i, carry):
            cols = pl.ds(pl.multiple_of(i * LC, LC), LC)
            dxs[rows_of(t), cols] = dot(ag[rows_of(t), hid : 2 * hid], up_ref[cols, :], 1, 1).astype(BF16)
            return carry

        lax.fori_loop(0, dl // LC, part, 0)
        dxs[rows_of(t), dl : dl + 128] = ag[rows_of(t), 2 * hid : 2 * hid + 128]

    def send_back(t):
        for o in range(1, NO):
            back_copy(t, o).start()
        dxr[t * BR : t * BR + TR, :] = dxs[t * BR : t * BR + TR, :]

    def token_sum(j, lo, hi_lane):
        total = None
        for t in range(TILES):
            if j in SPANS[t]:
                n = SPANS[t].index(j)
                one = dot(smat[rows_of(t), n * tok : (n + 1) * tok], dxr[rows_of(t), lo:hi_lane], 0, 0)
                total = one if total is None else total + one
        return total

    def score_sum(j):
        sums = [0.0, 0.0]
        for t in range(TILES):
            if j in SPANS[t]:
                value = dxr[rows_of(t), dl : dl + 128].astype(F32)
                for k, hit in enumerate(matches(t, j)):
                    sums[k] = sums[k] + jnp.sum(jnp.where(hit, value, 0.0), axis=0, keepdims=True)
        return jnp.where(line == 0, sums[0], jnp.where(line == 1, sums[1], 0.0))

    def lanes_of(way, m):
        return half_lanes if (way + m) % 2 else 0

    def sum_rows(way, m):
        return slice((way * 7 + m) * tok, (way * 7 + m + 1) * tok)

    def sum_copy(way, m):
        n = way * 7 + m
        rows = pl.ds(n * tok, tok if m else LAST)
        return remote(rso.at[rows, :], rsi.at[rows, :], rs_s.at[n], rs_r.at[n], {"ep": neighbour[way]})

    def score_copy(way, step):
        n = way * 4 + step
        rows = pl.ds(n * 8, 8)
        return remote(sco.at[rows, :], sci.at[rows, :], sc_s.at[n], sc_r.at[n], {"ep": neighbour[way]})

    def scored(way, step):
        return step > 0 or way == 0

    def sum_ready(way, m):
        lo = lanes_of(way, m)
        if m == 0:
            tf[way * tok : way * tok + LAST, :] = dot(
                pm[...], dxr[rows_of(TILES - 1), lo : lo + half_lanes], 0, 0
            )
            return
        tf[way * tok : (way + 1) * tok, :] = token_sum(FAR_TO_NEAR[way][(m + 1) // 2], lo, lo + half_lanes)

    def sum_next(way, m):
        count = tok if m else LAST
        total = tf[way * tok : way * tok + count, :]
        first = (way * 7 + m) * tok
        if m >= 2:
            sum_copy(way, m - 2).wait_recv()
        if m == 2:
            came = rsi[first - 2 * tok : first - 2 * tok + LAST, :]
            total = total + dot(lmat[(1 - way) * LAST : (2 - way) * LAST, :], came, 0, 0)
        elif m > 2:
            total = total + rsi[sum_rows(way, m - 2), :].astype(F32)
        rso[first : first + count, :] = total.astype(BF16)
        sum_copy(way, m).start()

    def score_next(way, step):
        n = way * 4 + step
        here = score_sum(FAR_TO_NEAR[way][step])
        if step > 0 and scored(way, step - 1):
            score_copy(way, step - 1).wait_recv()
            here = here + sci[n * 8 - 8 : n * 8, :]
        sco[n * 8 : n * 8 + 8, :] = here
        score_copy(way, step).start()

    def up_gradient():
        def part(i, carry):
            cols = pl.ds(pl.multiple_of(i * LC, LC), LC)
            gu_ref[cols, :] = dot(rx[0:slots, cols], ag[:, hid : 2 * hid], 0, 0).astype(BF16)
            return carry

        lax.fori_loop(0, dl // LC, part, 0)

    def down_gradient(first, last):
        def part(i, carry):
            cols = pl.ds(pl.multiple_of(i * LC, LC), LC)
            gd_ref[:, cols] = dot(ag[:, 0:hid], rx[slots : 2 * slots, cols], 0, 0).astype(BF16)
            return carry

        lax.fori_loop(first, last, part, 0)

    gather_start()
    gather_next(0, 0)
    select(0, 0)
    gather_next(0, 1)
    select(0, 1)
    gather_next(1, 0)
    select(1, 0)
    select(2, 0)
    slot_row = lax.broadcasted_iota(jnp.int32, (BR, LAST), 0)
    rank_row = (slot_row & 15) - (TR - CAP)
    spot_of = jnp.where(rank_row >= 0, (slot_row >> 4) * CAP + rank_row, -1)
    pm[...] = jnp.where(spot_of == lax.broadcasted_iota(jnp.int32, (BR, LAST), 1), 1.0, 0.0).astype(BF16)
    for load in loads:
        load.wait()
    hidden(0)
    chip_sum(0)
    gather_next(1, 1)
    select(1, 1)
    select(2, 1)
    activate(0)
    back_rows(0)
    gather_next(2, 0)
    select(3, 0)
    hidden(1)
    chip_sum(1)
    gather_next(2, 1)
    select(3, 1)
    activate(1)
    hidden(2)
    chip_sum(2)
    gather_copy(0, 3, 2).wait_recv()
    for h in range(2):
        for part in range(2):
            last_copy(part, h).wait_recv()
            select(4, part, h)
    hidden(3)
    chip_sum(3)
    hidden(4)
    chip_sum(4)
    activate(2)
    activate(3)
    back_rows(3)
    activate(4)
    send_back(3)
    back_rows(4)
    send_back(4)
    back_rows(2)
    send_back(2)
    back_rows(1)
    send_back(1)
    send_back(0)
    stores = [
        pltpu.make_async_copy(gu_ref, gu_hbm, w_s.at[2]),
        pltpu.make_async_copy(gd_ref, gd_hbm, w_s.at[3]),
    ]
    up_gradient()
    stores[0].start()
    back_all(4).wait_recv()
    for way in range(2):
        sum_ready(way, 0)
        sum_next(way, 0)
    back_all(3).wait_recv()
    for m in range(1, 7):
        if m == 3:
            back_all(2).wait_recv()
        for way in range(2):
            if (way, m) == (1, 3):
                back_all(1).wait_recv()
            if (way, m) == (1, 5):
                back_all(0).wait_recv()
            sum_ready(way, m)
            sum_next(way, m)
        if m == 1:
            down_gradient(0, 3)
        if m == 3:
            down_gradient(3, 5)
        if m == 4:
            down_gradient(5, dl // LC)
            stores[1].start()
        if m % 2 == 0:
            for way in range(2):
                if m == 2 and way == 0:
                    score_next(0, 0)
                score_next(way, m // 2)
    for n, lo in enumerate((0, half_lanes)):
        tf[n * tok : (n + 1) * tok, :] = token_sum(0, lo, lo + half_lanes)
    scores = score_sum(0)
    for m in (5, 6):
        for way in range(2):
            sum_copy(way, m).wait_recv()
    for m in (5, 6):
        lo = lanes_of(0, m)
        n = lo // half_lanes
        gx_ref[:, lo : lo + half_lanes] = (
            tf[n * tok : (n + 1) * tok, :]
            + rsi[sum_rows(0, m), :].astype(F32)
            + rsi[sum_rows(1, 11 - m), :].astype(F32)
        ).astype(BF16)
    for way in range(2):
        score_copy(way, 3).wait_recv()
    gates = jnp.where(line == 0, ma[2:3, :], jnp.where(line == 1, ma[3:4, :], 1.0))
    gs_ref[...] = ((scores + sci[24:32, :] + sci[56:64, :]) / gates)[0:2, :]

    for way in range(2):
        for step in range(4):
            for n in range(3):
                if gather_sent(way, step, n):
                    gather_copy(way, step, n).wait_send()
            if scored(way, step):
                score_copy(way, step).wait_send()
        for m in range(7):
            sum_copy(way, m).wait_send()
        for h in range(2):
            last_copy(way, h).wait_send()
    for t in range(TILES):
        for part in range(2):
            for copy in yx_all(t, part):
                copy.wait_send()
        back_all(t).wait_send()
        for stage in range(3):
            dp_copy(t, stage).wait_send()
    for store in stores:
        store.wait()


def hand_over(*refs):
    sems = refs[12]
    loads, stores = [], []
    for n in range(4):
        pieces = PIECES if refs[n].shape[0] % (16 * PIECES) == 0 else 1
        size = refs[n].shape[0] // pieces
        for i in range(pieces):
            rows = pl.ds(i * size, size)
            held = refs[8 + n].at[rows, :]
            loads.append(pltpu.make_async_copy(refs[n].at[rows, :], held, sems.at[0, n, i]))
            stores.append(pltpu.make_async_copy(held, refs[4 + n].at[rows, :], sems.at[1, n, i]))
    for load in loads:
        load.start()
    for load, store in zip(loads, stores):
        load.wait()
        store.start()
    for store in stores:
        store.wait()


def on_device(tokens, cotangent, gate_prob, expert_ids, w_up, w_down):
    tok, dl = tokens.shape
    hid = w_up.shape[2]
    vmem = pl.BlockSpec(memory_space=pltpu.VMEM)
    hbm = pl.BlockSpec(memory_space=pl.ANY)
    rows = TILES * BR
    halves = rows // 2
    wide = max(len(s) for s in SPANS) * tok
    scratch = [
        pltpu.VMEM((6 * tok, dl), BF16),
        pltpu.VMEM((6 * tok, dl), BF16),
        pltpu.VMEM((8 * 8, tok), F32),
        pltpu.VMEM((rows, wide), BF16),
        pltpu.VMEM((BR, wide), BF16),
        pltpu.VMEM((2 * rows, dl), BF16),
        pltpu.VMEM((2 * rows, dl), BF16),
        pltpu.VMEM((BR, 2 * hid), F32),
        pltpu.VMEM((halves, 2 * hid), F32),
        pltpu.VMEM((halves, 2 * hid), BF16),
        pltpu.VMEM((halves, 2 * hid), BF16),
        pltpu.VMEM((halves, 2 * hid), BF16),
        pltpu.VMEM((halves, 2 * hid), BF16),
        pltpu.VMEM((rows, 2 * hid + 128), BF16),
        pltpu.VMEM((rows, dl + 128), BF16),
        pltpu.VMEM((rows, dl + 128), BF16),
        pltpu.VMEM((14 * tok, dl // 2), BF16),
        pltpu.VMEM((14 * tok, dl // 2), BF16),
        pltpu.VMEM((8 * 8, tok), F32),
        pltpu.VMEM((8 * 8, tok), F32),
        pltpu.VMEM((2 * tok, dl // 2), F32),
        pltpu.VMEM((dl, hid), BF16),
        pltpu.VMEM((hid, dl), BF16),
        pltpu.VMEM((dl, hid), BF16),
        pltpu.VMEM((hid, dl), BF16),
        pltpu.VMEM((2 * LAST, tok), BF16),
        pltpu.VMEM((LAST, tok), BF16),
        pltpu.VMEM((2 * LAST, dl), BF16),
        pltpu.VMEM((2 * LAST, dl), BF16),
        pltpu.VMEM((BR, LAST), BF16),
    ]
    scratch += [
        pltpu.SemaphoreType.DMA((4,)),
        pltpu.SemaphoreType.DMA((4,)),
        pltpu.SemaphoreType.DMA((4,)),
    ]
    for count in (24, 2 * TILES + 2, 3 * TILES, TILES, 14, 8):
        scratch += [pltpu.SemaphoreType.DMA((count,))] * 2
    grad_tokens, scores, grad_up, grad_down = pl.pallas_call(
        kernel,
        out_shape=(
            jax.ShapeDtypeStruct((tok, dl), BF16),
            jax.ShapeDtypeStruct((2, tok), F32),
            jax.ShapeDtypeStruct((dl, hid), BF16),
            jax.ShapeDtypeStruct((hid, dl), BF16),
        ),
        in_specs=[vmem] * 4 + [hbm] * 2,
        out_specs=(vmem, vmem, hbm, hbm),
        scratch_shapes=scratch,
        compiler_params=pltpu.CompilerParams(
            collective_id=0, has_side_effects=True, vmem_limit_bytes=60 * 2**20
        ),
    )(tokens, cotangent, gate_prob.T, expert_ids.T, w_up[0], w_down[0])
    made = (grad_tokens, scores, grad_up, grad_down)
    grad_tokens, scores, grad_up, grad_down = pl.pallas_call(
        hand_over,
        out_shape=tuple(jax.ShapeDtypeStruct(a.shape, a.dtype) for a in made),
        in_specs=[hbm] * 4,
        out_specs=(hbm,) * 4,
        scratch_shapes=[pltpu.VMEM(a.shape, a.dtype) for a in made] + [pltpu.SemaphoreType.DMA((2, 4, PIECES))],
    )(*made)
    return grad_tokens, scores.T, grad_up[None], grad_down[None]


def solution(mesh):
    in_specs = (
        P("ep", "dp"),
        P("ep", "dp"),
        P("ep", None),
        P("ep", None),
        P("ep", "dp", None),
        P("ep", None, "dp"),
    )
    out_specs = (P("ep", "dp"), P("ep", None), P("ep", "dp", None), P("ep", None, "dp"))
    return jax.shard_map(
        on_device, mesh=mesh, in_specs=in_specs, out_specs=out_specs, check_vma=False
    )
```
